32 devices in a mesh: tok: 8 (over y, x, core), feat: 4 (over z).
Axes of the slice: x: 2, y: 2, z: 4, core: 2. Of those that a mesh axis runs over, the one named last changes fastest.
Arguments:
- inputs: bfloat16 [2048, 2048], P(('tok', 'feat'))
- norm_gain: float32 [2048], replicated, may hold values from 0.1 to 1.9
- w_in: bfloat16 [512, 8192], P('tok', 'feat'), may hold values from -0.25 to 0.25
- w_out: bfloat16 [512, 8192], P('tok', 'feat'), may hold values from -0.125 to 0.125
- block_index: int32 [64, 4], P('feat'), may hold values from 0 to 15, all different within a row
- segment_ids: int32 [2048], P(('tok', 'feat')), may hold values from 0 to 127, never falling along the last dimension, each value on 1 to 24 neighbouring positions
- teacher_scores: float32 [128], replicated, may hold values from -6 to 6
- upstream: bfloat16 [2048, 2048], P(('tok', 'feat')), may hold values from -6 to 6
- readout: float32 [2048], replicated, may hold values from -0.125 to 0.125
Outputs:
- layer_out: bfloat16 [2048, 2048], P(('tok', 'feat'))
- input_grad: bfloat16 [2048, 2048], P(('tok', 'feat'))
- grad_in: float32 [512, 8192], P('tok', 'feat')
- grad_out: float32 [512, 8192], P('tok', 'feat')
The draws below stay inside these ranges and needn't reach their ends.
Inputs may be any that keep to these rules, and one draw needn't show every extreme that they name: `block_index`: each row names 4 different feature blocks; every feature block is named by some row. `segment_ids`: never falls along the tokens; every segment 0 to 127 holds 1 to 24 tokens.
All inputs are finite; a program needn't handle non-finite values.
Results may differ from the reference program's by a relative error of at most 0.015.
Values may be sent and summed in bfloat16 or wider, within the bound.
No kernel may reach another device: no remote copies, remote signals or barrier semaphores. Data moves between devices by JAX's collectives and lax.ppermute only.
A program may use at most 128 MiB of HBM per device.

```python
import math
import jax
import jax.numpy as jnp
import numpy as np
from jax import lax

D = 2048
FF = 8192
BLK = 128
SEG_MOST = 24
TOK_DEV = 64
KB = 4
TOKENS = 2048
NSEG = 128
N_TOK = 8
N_FEAT = 4


def draw_inputs(key, part):
    first, second, third = jax.random.split(key, 3)
    base = jax.random.normal(first, (TOKENS, D), jnp.float32)
    row_scale = 0.5 * jnp.exp(jax.random.uniform(second, (TOKENS, 1), jnp.float32, 0.0, math.log(10.0)))
    col_scale = jnp.exp(jax.random.uniform(third, (1, D), jnp.float32, math.log(0.5), math.log(2.0)))
    return (base * row_scale * col_scale).astype(jnp.bfloat16)


def level_of(own_key, extent, cuts, smallest, top_value):
    loudness = 1.0
    for dim, blocks in cuts:
        steps = jax.random.uniform(jax.random.fold_in(jax.random.fold_in(own_key, 6), dim), (blocks,), jnp.float32, smallest / len(cuts), top_value / len(cuts))
        loudness = loudness * jnp.repeat(jnp.exp(steps), extent[dim] // blocks).reshape((-1,) + (1,) * (len(extent) - 1 - dim))
    return loudness


def different_ones(own_key, rows, amount, top, lift):
    sequence = jax.random.permutation(jax.random.fold_in(own_key, 1), amount)
    pull = sequence
    for power in range(3):
        pull = pull * pull // amount
    pull = pull * lift // amount
    lots = jax.random.randint(jax.random.fold_in(own_key, 2), (rows, amount), 0, 4096) + pull
    holders = jax.random.permutation(jax.random.fold_in(own_key, 3), rows)[jnp.arange(amount) % rows]
    lots = jnp.where(jnp.arange(rows)[:, None] == holders[None, :], 1 << 14, lots)
    merit = lots * amount + jnp.arange(amount)
    return lax.top_k(merit.astype(jnp.int32), top)[1].astype(jnp.int32)


def profile(amount, total, bound, skew):
    loads = [(1 << 20) // math.isqrt(standing ** skew) + 1 for standing in range(2, amount + 1)]
    rest, given = total - bound - (amount - 1), [1] * (amount - 1)
    while rest > 0:
        movable = [i for i in range(amount - 1) if given[i] < bound]
        whole, budget = sum([loads[i] for i in movable]), rest
        for i in movable:
            more = min(bound - given[i], max(1, budget * loads[i] // whole), rest)
            given[i] = given[i] + more
            rest = rest - more
    return np.array([bound] + given)


def uneven_parts(stream_key, amount, total, most, skew):
    if amount == 2:
        one = jax.random.randint(stream_key, (), max(1, total - most), min(most, total - 1) + 1)
        return jnp.stack([one, total - one])
    tallies = jnp.asarray(profile(amount, total, most, skew), jnp.int32)
    pairs = (amount - 1) // 2
    donor, sink = tallies[1:1 + 2 * pairs:2], tallies[2:2 + 2 * pairs:2]
    slack = jnp.minimum(donor - 1, most - sink)
    passed = jax.random.randint(jax.random.fold_in(stream_key, 1), (pairs,), 0, 1 << 20) % (slack + 1)
    tallies = tallies.at[1:1 + 2 * pairs:2].set(donor - passed).at[2:2 + 2 * pairs:2].set(sink + passed)
    return tallies[jax.random.permutation(jax.random.fold_in(stream_key, 2), amount)]


def bell_draw(key, dims, deviation, reach, cuts=(), held_as=jnp.bfloat16):
    entries = deviation * jax.random.normal(key, dims, jnp.float32)
    if cuts:
        entries = entries * level_of(key, dims, cuts, -0.22, 0.18)
    return jnp.clip(entries, -reach, reach).astype(held_as)


def setup_inputs(seed: int = 0) -> dict:
    key_of = jax.random.split(jax.random.key(seed), 10)
    return {
        "inputs": draw_inputs(jax.random.fold_in(key_of[9], 71), 0),
        "norm_gain": jnp.clip(1.0 + 0.18 * jax.random.normal(key_of[1], (D,), jnp.float32), 0.1, 1.9),
        "w_in": bell_draw(key_of[2], (KB * BLK, FF), (KB * BLK) ** -0.5, 0.25, ((0, 8), (1, 4))),
        "w_out": bell_draw(key_of[3], (KB * BLK, FF), (FF * KB // (D // BLK)) ** -0.5, 0.125, ((0, 8), (1, 4))),
        "block_index": different_ones(key_of[4], (FF // BLK), D // BLK, KB, 2048),
        "segment_ids": jnp.searchsorted(jnp.cumsum(uneven_parts(key_of[5], NSEG, TOKENS, SEG_MOST, 1)), jnp.arange(TOKENS), side="right").astype(jnp.int32),
        "teacher_scores": bell_draw(key_of[6], (NSEG,), 1.0, 6.0, (), jnp.float32),
        "upstream": bell_draw(key_of[7], (TOKENS, D), 1.0, 6.0, ((0, 32),)),
        "readout": bell_draw(key_of[8], (D,), D ** -0.5, 0.125, (), jnp.float32),
    }


EPS = 1e-06
LOSS_WEIGHT = 8.0
HIGHEST = lax.Precision.HIGHEST

def gelu_tanh(values):
    return jax.nn.gelu(values, approximate=True)

def gelu_back(values, cotangent):
    return jax.vjp(gelu_tanh, values)[1](cotangent)[0]

def rounded(values):
    return lax.optimization_barrier(values.astype(jnp.bfloat16)).astype(jnp.float32)

def reference(inputs, norm_gain, w_in, w_out, block_index, segment_ids, teacher_scores, upstream, readout):
    feature_blocks = D // BLK
    hidden_blocks = FF // BLK
    group_blocks = hidden_blocks // N_FEAT
    picked_width = KB * BLK
    group_rows = TOK_DEV * N_FEAT
    selector = (block_index[:, :, None] == jnp.arange(feature_blocks, dtype=jnp.int32)[None, None, :]).astype(jnp.float32)
    sel_groups = selector.reshape(N_FEAT, group_blocks, KB, feature_blocks)
    w_in_blocks = w_in.astype(jnp.float32).reshape(picked_width, hidden_blocks, BLK)
    w_out_blocks = w_out.astype(jnp.float32).reshape(picked_width, hidden_blocks, BLK)
    inputs_wide = inputs.astype(jnp.float32)
    inv_rms = lax.rsqrt(lax.optimization_barrier(jnp.mean(inputs_wide * inputs_wide, axis=1, keepdims=True)) + EPS)
    normed = (inputs_wide * inv_rms * norm_gain[None, :]).astype(jnp.bfloat16)

    def select(rows):
        blocks = rows.astype(jnp.float32).reshape(group_rows, feature_blocks, BLK)
        picked = jnp.einsum('rdc,jkd->rjkc', blocks, selector, precision=HIGHEST)
        return picked.reshape(group_rows, hidden_blocks, picked_width)

    def spread(terms):
        grouped = terms.reshape(group_rows, N_FEAT, group_blocks, KB, BLK)
        parts = jnp.einsum('rgjkc,gjkd->rgdc', grouped, sel_groups, precision=HIGHEST)
        return lax.optimization_barrier(jnp.sum(rounded(parts), axis=1)).reshape(group_rows, D)

    def forward_group(rows):
        pre_act = jnp.einsum('rjm,mjc->rjc', select(rows), w_in_blocks, precision=HIGHEST)
        activated = rounded(gelu_tanh(pre_act))
        terms = jnp.einsum('rjc,mjc->rjm', activated, w_out_blocks, precision=HIGHEST)
        return spread(terms)
    normed_groups = normed.reshape(N_TOK, group_rows, D)
    branch = lax.map(forward_group, normed_groups).reshape(TOKENS, D)
    layer_out = (inputs_wide + branch).astype(jnp.bfloat16)
    token_score = jnp.dot(layer_out.astype(jnp.float32), readout, precision=HIGHEST)
    score_sums = jax.ops.segment_sum(token_score, segment_ids, num_segments=NSEG)
    token_counts = jax.ops.segment_sum(jnp.ones_like(token_score), segment_ids, num_segments=NSEG)
    misfit = score_sums / token_counts - teacher_scores
    token_coeff = 2.0 * LOSS_WEIGHT * misfit[segment_ids]
    cotangent = (upstream.astype(jnp.float32) + token_coeff[:, None] * readout[None, :]).astype(jnp.bfloat16)

    def backward_group(totals, items):
        rows, grads = items
        chosen = select(rows)
        pre_act = jnp.einsum('rjm,mjc->rjc', chosen, w_in_blocks, precision=HIGHEST)
        activated = rounded(gelu_tanh(pre_act))
        chosen_grad = select(grads)
        upper_grad = jnp.einsum('rjm,mjc->rjc', chosen_grad, w_out_blocks, precision=HIGHEST)
        pre_grad = rounded(gelu_back(pre_act, upper_grad))
        back_terms = jnp.einsum('rjc,mjc->rjm', pre_grad, w_in_blocks, precision=HIGHEST)
        in_terms = jnp.einsum('rjm,rjc->mjc', chosen, pre_grad, precision=HIGHEST)
        out_terms = jnp.einsum('rjm,rjc->mjc', chosen_grad, activated, precision=HIGHEST)
        return ((totals[0] + in_terms, totals[1] + out_terms), spread(back_terms))
    zero_grads = jnp.zeros((picked_width, hidden_blocks, BLK), jnp.float32)
    cot_groups = cotangent.reshape(N_TOK, group_rows, D)
    (in_total, out_total), back = lax.scan(backward_group, (zero_grads, zero_grads), (normed_groups, cot_groups))
    back = back.reshape(TOKENS, D)
    scaled = back * norm_gain[None, :]
    inner_mean = lax.optimization_barrier(jnp.mean(scaled * inputs_wide, axis=1, keepdims=True))
    norm_back = inv_rms * scaled - inputs_wide * (inv_rms * inv_rms * inv_rms) * inner_mean
    input_grad = (cotangent.astype(jnp.float32) + norm_back).astype(jnp.bfloat16)
    grad_scale = 1.0 / math.sqrt(TOKENS)
    grad_in = in_total.reshape(picked_width, FF) * grad_scale
    grad_out = out_total.reshape(picked_width, FF) * grad_scale
    return (layer_out, input_grad, grad_in, grad_out)
```

```python
import functools
import math

import jax
import jax.numpy as jnp
from jax import lax
from jax.experimental import pallas as pl
from jax.experimental.pallas import tpu as pltpu
from jax.sharding import PartitionSpec as P

BLK = 128
EPS = 1e-06
LOSS_WEIGHT = 8.0
GELU_A = math.sqrt(2.0 / math.pi)
GELU_B = 0.044715
VMEM_BYTES = 48 * 1024 * 1024
BF16 = jnp.bfloat16
F32 = jnp.float32
NT = (((1,), (1,)), ((), ()))
TN = (((0,), (0,)), ((), ()))


def dot(a, b, dims=(((1,), (0,)), ((), ()))):
    return lax.dot_general(a, b, dims, preferred_element_type=F32)


def three_terms(row):
    hi = row.astype(BF16)
    rest = row - hi.astype(F32)
    mid = rest.astype(BF16)
    low = (rest - mid.astype(F32)).astype(BF16)
    pad = jnp.zeros((8 - 3, row.shape[1]), F32).astype(BF16)
    return jnp.concatenate([hi, mid, low, pad], axis=0)


def forward_kernel(masks_in, masks_out, nf, *refs):
    idx, place = refs[0], refs[1]
    refs = refs[2:]
    xs, refs = refs[:nf], refs[nf:]
    gain, readout = refs[:2]
    refs = refs[2:]
    win_parts, refs = refs[: len(masks_in)], refs[len(masks_in):]
    wout_parts, refs = refs[: len(masks_out)], refs[len(masks_out):]
    normed, act, dact, win, wout, score = refs[:6]
    branch, acc = refs[6 : 6 + nf], refs[6 + nf]
    rows = xs[0].shape[0]
    fb = normed.shape[0]
    nj, kb = idx.shape
    for d in range(nf):
        x = xs[d][...].astype(F32)
        inv = lax.rsqrt(jnp.mean(x * x, axis=1, keepdims=True) + EPS)
        n = (x * inv * gain[...]).astype(BF16)
        for b in range(fb):
            normed[b, d * rows : (d + 1) * rows, :] = n[:, b * BLK : (b + 1) * BLK]
    for parts, masks, whole in ((win_parts, masks_in, win), (wout_parts, masks_out, wout)):
        for part, ms in zip(parts, masks):
            depth = part.shape[0] // len(ms)
            for i, m in enumerate(ms):
                at = pl.multiple_of((place[0] ^ m) * depth, depth)
                for j in range(nj):
                    whole[j, pl.ds(at, depth), :] = part[
                        i * depth : (i + 1) * depth, j * BLK : (j + 1) * BLK
                    ]
    acc[...] = jnp.zeros_like(acc)

    @pl.loop(0, nj)
    def _(j):
        which = [idx[j, k] for k in range(kb)]
        picked = jnp.concatenate([normed[w] for w in which], axis=1)
        v = dot(picked, win[j])
        v2 = v * v
        t = jnp.tanh(GELU_A * v * (1.0 + GELU_B * v2))
        half = 0.5 * (1.0 + t)
        a = (v * half).astype(BF16)
        act[j] = a
        dact[j] = half + 0.5 * v * (1.0 - t * t) * (GELU_A * (1.0 + 3.0 * GELU_B * v2))
        terms = dot(a, wout[j], NT)
        for k, w in enumerate(which):
            acc[w] += terms[:, k * BLK : (k + 1) * BLK]

    total = jnp.zeros((8, nf * rows), F32)
    own = jnp.zeros((8, rows), F32)
    for b in range(fb):
        part = acc[b].astype(BF16)
        r = three_terms(readout[:, b * BLK : (b + 1) * BLK])
        total = total + dot(r, part, NT)
        own = own + dot(r, xs[0][:, b * BLK : (b + 1) * BLK], NT)
        for d in range(nf):
            branch[d][:, b * BLK : (b + 1) * BLK] = part[d * rows : (d + 1) * rows]
    own = jnp.sum(own, axis=0, keepdims=True)
    pad = jnp.zeros((1, (nf - 1) * rows), F32)
    score[...] = jnp.sum(total, axis=0, keepdims=True) + jnp.concatenate([own, pad], axis=1)


def backward_kernel(nf, *refs):
    idx = refs[0]
    ups, refs = refs[1 : 1 + nf], refs[1 + nf:]
    score, sleft, sright, ids, ileft, iright, teacher, readout = refs[:8]
    win, wout, dact, cot, pre_grad, own_cot = refs[8:14]
    back, acc = refs[14 : 14 + nf], refs[14 + nf]
    rows = ups[0].shape[0]
    fb = cot.shape[0]
    nj, kb = idx.shape
    tokens = nf * rows
    nseg = teacher.shape[0]
    seg = lax.broadcasted_iota(jnp.int32, (nseg, tokens), 0) + 1
    sums = jnp.zeros((nseg, 1), F32)
    counts = jnp.zeros((nseg, 1), F32)
    for s, i in ((score, ids), (sleft, ileft), (sright, iright)):
        here = i[...] == seg
        sums = sums + jnp.sum(jnp.where(here, s[...], 0.0), axis=1, keepdims=True)
        counts = counts + jnp.sum(jnp.where(here, 1.0, 0.0), axis=1, keepdims=True)
    misfit = sums / jnp.maximum(counts, 1.0) - teacher[...]
    coeff = 2.0 * LOSS_WEIGHT * jnp.sum(
        jnp.where(ids[...] == seg, misfit, 0.0), axis=0, keepdims=True
    )
    column = jnp.transpose(jnp.broadcast_to(coeff, (BLK, tokens)))
    for d in range(nf):
        for b in range(fb):
            c = (
                ups[d][:, b * BLK : (b + 1) * BLK].astype(F32)
                + column[d * rows : (d + 1) * rows] * readout[:, b * BLK : (b + 1) * BLK]
            ).astype(BF16)
            cot[b, d * rows : (d + 1) * rows, :] = c
            if d == 0:
                own_cot[:, b * BLK : (b + 1) * BLK] = c
    acc[...] = jnp.zeros_like(acc)

    @pl.loop(0, nj)
    def _(j):
        which = [idx[j, k] for k in range(kb)]
        picked = jnp.concatenate([cot[w] for w in which], axis=1)
        p = (dot(picked, wout[j]) * dact[j]).astype(BF16)
        pre_grad[j] = p
        terms = dot(p, win[j], NT)
        for k, w in enumerate(which):
            acc[w] += terms[:, k * BLK : (k + 1) * BLK]

    for b in range(fb):
        part = acc[b].astype(BF16)
        for d in range(nf):
            back[d][:, b * BLK : (b + 1) * BLK] = part[d * rows : (d + 1) * rows]


def grads_kernel(orders, scale, idx, place, cot, act, normed, pre_grad, *outs):
    nj, kb = idx.shape
    n = len(orders[0])
    depth = kb * BLK // n
    half = n // 2

    def one(left, right, keep, send, order, j):
        at = [0] * n
        for pos, m in enumerate(order):
            at[m] = pos
        for k in range(kb):
            g = (dot(left[idx[j, k]], right[j], TN) * scale).astype(BF16)
            for part in range(BLK // depth):
                owner = k * (BLK // depth) + part
                m = place[0] ^ owner
                pos = at[n - 1]
                for c in range(n - 1):
                    pos = jnp.where(m == c, at[c], pos)
                piece = g[part * depth : (part + 1) * depth]
                col = pl.ds(pl.multiple_of(j * BLK, BLK), BLK)

                @pl.when(pos < half)
                def _():
                    keep[pl.ds(pl.multiple_of(pos * depth, depth), depth), col] = piece

                @pl.when(pos >= half)
                def _():
                    send[pl.ds(pl.multiple_of((pos - half) * depth, depth), depth), col] = piece

    @pl.loop(0, nj)
    def _(j):
        one(cot, act, outs[0], outs[1], orders[0], j)
        one(normed, pre_grad, outs[2], outs[3], orders[1], j)


def finish_kernel(x_ref, gain, cot, own, *refs):
    others, out = refs[:-1], refs[-1]
    x = x_ref[...].astype(F32)
    inv = lax.rsqrt(jnp.mean(x * x, axis=1, keepdims=True) + EPS)
    total = own[...].astype(F32)
    for o in others:
        total = total + o[...].astype(F32)
    g = total * gain[...]
    inner = jnp.mean(g * x, axis=1, keepdims=True)
    out[...] = (cot[...].astype(F32) + (inv * g - x * (inv * inv * inv) * inner)).astype(BF16)


VM = pl.BlockSpec(memory_space=pltpu.VMEM)
SM = pl.BlockSpec(memory_space=pltpu.SMEM)


def call(body, outs, args, scalars, scratch, flops):
    return pl.pallas_call(
        body,
        out_shape=outs,
        in_specs=[SM] * scalars + [VM] * (len(args) - scalars),
        out_specs=[VM] * len(outs),
        scratch_shapes=scratch,
        compiler_params=pltpu.CompilerParams(vmem_limit_bytes=VMEM_BYTES),
        cost_estimate=pl.CostEstimate(
            flops=flops,
            bytes_accessed=sum(math.prod(o.shape) * o.dtype.itemsize for o in outs),
            transcendentals=0,
        ),
    )(*args)


def xor(n, mask):
    return [(i, i ^ mask) for i in range(n)]


def swap(value, axis, mask):
    return lax.ppermute(value, axis, xor(lax.axis_size(axis), mask))


def bits_of(n):
    return [1 << b for b in range(n.bit_length() - 1)]


def gather_tok(w, bits):
    held, masks = [w], [[0]]
    for bit in bits:
        whole = jnp.concatenate(held, axis=0) if len(held) > 1 else held[0]
        flat = [m for ms in masks for m in ms]
        held, masks = [whole, swap(whole, "tok", bit)], [flat, [m ^ bit for m in flat]]
    other = [swap(h, "tok", 1) for h in held]
    return held + other, masks + [[m ^ 1 for m in ms] for ms in masks]


def order_of(bits):
    order = [0]
    for bit in reversed(bits):
        order = order + [m ^ bit for m in order]
    return order


def scatter_tok(keep, send, bits):
    total = keep.astype(F32) + swap(send, "tok", bits[0]).astype(F32)
    for bit in bits[1:]:
        half = total.shape[0] // 2
        total = total[:half] + swap(total[half:].astype(BF16), "tok", bit).astype(F32)
    return total


def on_device(
    inputs, norm_gain, w_in, w_out, block_index, segment_ids, teacher_scores, upstream, readout
):
    rows, width = inputs.shape
    nt, nf = lax.axis_size("tok"), lax.axis_size("feat")
    nj, kb = block_index.shape
    hidden = w_in.shape[1]
    fb = width // BLK
    tokens = rows * nf
    grad_scale = 1.0 / math.sqrt(tokens * nt)
    tok_bits = bits_of(nt)
    feat_bits = bits_of(nf)
    place = lax.axis_index("tok").astype(jnp.int32).reshape(1)
    gain_row, readout_row = norm_gain.reshape(1, width), readout.reshape(1, width)
    flops = 2 * tokens * hidden * kb * BLK

    win_parts, masks_in = gather_tok(w_in, tok_bits[1:])
    wout_parts, masks_out = gather_tok(w_out, tok_bits[1:][::-1])
    xs = [inputs] + [swap(inputs, "feat", d) for d in range(1, nf)]

    ids = segment_ids + 1
    for bit in feat_bits:
        ids = jnp.concatenate([ids, swap(ids, "feat", bit)])
    up_line = [(i, i + 1) for i in range(nt - 1)]
    down_line = [(i + 1, i) for i in range(nt - 1)]
    ids_left = lax.ppermute(ids, "tok", up_line)
    ids_right = lax.ppermute(ids, "tok", down_line)

    ups = [upstream] + [swap(upstream, "feat", d) for d in range(1, nf)]

    sds = jax.ShapeDtypeStruct
    piece = sds((rows, width), BF16)
    outs = call(
        functools.partial(forward_kernel, masks_in, masks_out, nf),
        [
            sds((fb, tokens, BLK), BF16),
            sds((nj, tokens, BLK), BF16),
            sds((nj, tokens, BLK), F32),
            sds((nj, kb * BLK, BLK), BF16),
            sds((nj, kb * BLK, BLK), BF16),
            sds((1, tokens), F32),
        ]
        + [piece] * nf,
        [block_index, place] + xs + [gain_row, readout_row] + win_parts + wout_parts,
        2,
        [pltpu.VMEM((fb, tokens, BLK), F32)],
        2 * flops,
    )
    normed, act, dact, win, wout, score = outs[:6]
    branch = outs[6:]

    score = score.reshape(nf, rows)
    for bit in feat_bits:
        score = score + jnp.flip(
            swap(score, "feat", bit).reshape(nf // (2 * bit), 2, bit, rows), axis=1
        ).reshape(nf, rows)
    score = score.reshape(1, tokens)
    score_left = lax.ppermute(score, "tok", up_line)
    score_right = lax.ppermute(score, "tok", down_line)

    total = branch[0].astype(F32)
    for d in range(1, nf):
        total = total + swap(branch[d], "feat", d).astype(F32)
    layer_out = (inputs.astype(F32) + total).astype(BF16)

    outs = call(
        functools.partial(backward_kernel, nf),
        [sds((fb, tokens, BLK), BF16), sds((nj, tokens, BLK), BF16), piece] + [piece] * nf,
        [block_index]
        + ups
        + [score, score_left, score_right]
        + [i.reshape(1, tokens) for i in (ids, ids_left, ids_right)]
        + [teacher_scores.reshape(-1, 1), readout_row, win, wout, dact],
        1,
        [pltpu.VMEM((fb, tokens, BLK), F32)],
        2 * flops,
    )
    cot, pre_grad, own_cot = outs[:3]
    back = outs[3:]
    back_others = [swap(back[d], "feat", d) for d in range(1, nf)]

    out_bits = [1] + tok_bits[1:]
    in_bits = [1] + tok_bits[1:][::-1]
    half = sds((kb * BLK // 2, hidden), BF16)
    keep_out, send_out, keep_in, send_in = call(
        functools.partial(grads_kernel, (order_of(out_bits), order_of(in_bits)), grad_scale),
        [half] * 4,
        [block_index, place, cot, act, normed, pre_grad],
        2,
        [],
        2 * flops,
    )
    grad_out = scatter_tok(keep_out, send_out, out_bits)
    grad_in = scatter_tok(keep_in, send_in, in_bits)
    (input_grad,) = call(
        finish_kernel,
        [piece],
        [inputs, gain_row, own_cot, back[0]] + back_others,
        0,
        [],
        rows * width,
    )
    return (layer_out, input_grad, grad_in, grad_out)


def solution(mesh):
    return jax.shard_map(
        on_device,
        mesh=mesh,
        in_specs=(
            P(("tok", "feat"), None),
            P(),
            P("tok", "feat"),
            P("tok", "feat"),
            P("feat", None),
            P(("tok", "feat")),
            P(),
            P(("tok", "feat"), None),
            P(),
        ),
        out_specs=(
            P(("tok", "feat"), None),
            P(("tok", "feat"), None),
            P("tok", "feat"),
            P("tok", "feat"),
        ),
        check_vma=False,
    )
```

```python
import functools
import math

import jax
import jax.numpy as jnp
from jax import lax
from jax.experimental import pallas as pl
from jax.experimental.pallas import tpu as pltpu
from jax.sharding import PartitionSpec as P

BLK = 128
EPS = 1e-06
LOSS_WEIGHT = 8.0
GELU_A = math.sqrt(2.0 / math.pi)
GELU_B = 0.044715
VMEM_BYTES = 32 * 1024 * 1024
BF16 = jnp.bfloat16
F32 = jnp.float32
NN = (((1,), (0,)), ((), ()))
NT = (((1,), (1,)), ((), ()))
TN = (((0,), (0,)), ((), ()))


def dot(a, b, dims=NN):
    return lax.dot_general(a, b, dims, preferred_element_type=F32)


def block(b):
    return slice(b * BLK, (b + 1) * BLK)


def column(j):
    return pl.ds(pl.multiple_of(j * BLK, BLK), BLK)


def bits_of(n):
    return [1 << b for b in range(n.bit_length() - 1)]


def three_terms(row):
    hi = row.astype(BF16)
    rest = row - hi.astype(F32)
    mid = rest.astype(BF16)
    low = (rest - mid.astype(F32)).astype(BF16)
    pad = jnp.zeros((8 - 3, row.shape[1]), F32).astype(BF16)
    return jnp.concatenate([hi, mid, low, pad], axis=0)


def load_weight(place, parts, masks, which, whole, sem):
    core = place[0] & 1
    for part, ms in zip(parts, masks):
        depth = part.shape[0] // (2 * len(ms))
        for i, (even, odd) in enumerate(ms):
            owner = place[0] ^ jnp.where(core == 0, even, odd)
            at = pl.multiple_of(owner * depth, depth)
            pltpu.make_async_copy(
                part.at[pl.ds((2 * i + which) * depth, depth)], whole.at[pl.ds(at, depth)], sem
            ).start()
    return lambda: pltpu.make_async_copy(whole, whole, sem).wait()


def load(src, dst, sem):
    copy = pltpu.make_async_copy(src, dst, sem)
    copy.start()
    return copy.wait


def loop(nj, unroll=4):
    return pl.loop(0, nj, unroll=math.gcd(nj, unroll))


def spread(acc, outs, rows):
    for b in range(acc.shape[0]):
        part = acc[b].astype(BF16)
        for d, out in enumerate(outs):
            out[:, block(b)] = part[d * rows : (d + 1) * rows]


def forward_kernel(masks, nf, *refs):
    idx, place = refs[:2]
    xs, refs = refs[2 : 2 + nf], refs[2 + nf:]
    gain, readout, ids = refs[:3]
    parts, refs = refs[3 : 3 + len(masks)], refs[3 + len(masks):]
    normed_out, act_out, dact_out, score = refs[:4]
    branch_out, refs = refs[4 : 4 + nf], refs[4 + nf:]
    xbuf, normed, act, dact, win, wout, acc, branch, sems = refs
    rows = ids.shape[1]
    fb = normed.shape[0]
    nj, kb = idx.shape
    waits = [load(xs[d], xbuf.at[d], sems.at[d]) for d in range(nf)]
    win_wait = load_weight(place, parts, masks, 0, win, sems.at[nf])
    wout_wait = load_weight(place, parts, masks, 1, wout, sems.at[nf + 1])
    acc[...] = jnp.zeros_like(acc)
    own = jnp.zeros((8, rows), F32)
    for d in range(nf):
        waits[d]()
        x = xbuf[d].astype(F32)
        inv = lax.rsqrt(jnp.mean(x * x, axis=1, keepdims=True) + EPS)
        n = (x * inv * gain[...]).astype(BF16)
        for b in range(fb):
            normed[b, d * rows : (d + 1) * rows, :] = n[:, block(b)]
            if d == 0:
                own = own + dot(three_terms(readout[:, block(b)]), xbuf[0, :, block(b)], NT)
    normed_wait = load(normed, normed_out, sems.at[nf + 2])
    win_wait()
    wout_wait()

    @loop(nj)
    def _(j):
        which = [idx[j, k] for k in range(kb)]
        picked = jnp.concatenate([normed[w] for w in which], axis=1)
        v = dot(picked, win[:, column(j)])
        v2 = v * v
        t = jnp.tanh(GELU_A * v * (1.0 + GELU_B * v2))
        half = 0.5 * (1.0 + t)
        a = (v * half).astype(BF16)
        act[j] = a
        dact[j] = half + 0.5 * v * (1.0 - t * t) * (GELU_A * (1.0 + 3.0 * GELU_B * v2))
        terms = dot(a, wout[:, column(j)], NT)
        for k, w in enumerate(which):
            acc[w] += terms[:, block(k)]

    act_wait = load(act, act_out, sems.at[nf + 3])
    dact_wait = load(dact, dact_out, sems.at[nf + 4])
    spread(acc, [branch.at[d] for d in range(nf)], rows)
    waits = [load(branch.at[d], branch_out[d], sems.at[d]) for d in range(nf)]
    total = jnp.zeros((8, nf * rows), F32)
    for b in range(fb):
        total = total + dot(three_terms(readout[:, block(b)]), acc[b].astype(BF16), NT)
    own = jnp.sum(own, axis=0, keepdims=True)
    pad = jnp.zeros((1, (nf - 1) * rows), F32)
    row = jnp.sum(total, axis=0, keepdims=True) + jnp.concatenate([own, pad], axis=1)
    score[...] = jnp.concatenate([row, ids[...].astype(F32) + 1.0], axis=1)
    for wait in waits + [normed_wait, act_wait, dact_wait]:
        wait()


def store_grads(idx, place, orders, scale, left, right, keep, send):
    nj, kb = idx.shape
    count = 2 << len(orders[0])
    depth = kb * BLK // count
    per = BLK // depth
    core = place[0] & 1

    def slot(owner, order):
        m = place[0] ^ owner
        pos = 0
        for bit in order:
            pos = 2 * pos + jnp.where((m & bit) != 0, 1, 0)
        return pos * depth

    def slots(own):
        return [
            pl.multiple_of(jnp.where(own == 0, slot(2 * q, orders[0]), slot(2 * q, orders[1])), depth)
            for q in range(count // 2)
        ]

    keep_at, send_at = slots(core), slots(1 - core)

    @loop(nj)
    def _(j):
        for k in range(kb):
            g = (dot(left[idx[j, k]], right[j], TN) * scale).astype(BF16)
            for half in range(per // 2):
                q = k * (per // 2) + half
                even = g[2 * half * depth : (2 * half + 1) * depth]
                odd = g[(2 * half + 1) * depth : (2 * half + 2) * depth]
                keep[pl.ds(keep_at[q], depth), column(j)] = jnp.where(core == 0, even, odd)
                send[pl.ds(send_at[q], depth), column(j)] = jnp.where(core == 0, odd, even)


def upper_kernel(masks, nf, *refs):
    idx, place = refs[:2]
    ups, refs = refs[2 : 2 + nf], refs[2 + nf:]
    readout, refs = refs[0], refs[1:]
    parts, refs = refs[: len(masks)], refs[len(masks):]
    upper_out, turn, pattern, ubuf, up, wout, upper, flat, sems = refs
    nj, kb = idx.shape
    fb = up.shape[0]
    rows = ubuf.shape[1]
    depth = pattern.shape[0]
    waits = [load(ups[d], ubuf.at[d], sems.at[d]) for d in range(nf)]
    wout_wait = load_weight(place, parts, masks, 1, wout, sems.at[nf])
    for d in range(nf):
        waits[d]()
        for b in range(fb):
            up[b, d * rows : (d + 1) * rows, :] = ubuf[d, :, block(b)]
    wout_wait()

    @loop(nj)
    def _(j):
        which = [idx[j, k] for k in range(kb)]
        picked = jnp.concatenate([up[w] for w in which], axis=1)
        upper[j] = dot(picked, wout[:, column(j)])
        pltpu.make_async_copy(upper.at[j], upper_out.at[j], sems.at[nf + 1]).start()
        turned = jnp.concatenate([three_terms(readout[:, column(w)]) for w in which], axis=1)
        turn[:, column(j)] = jnp.sum(dot(turned, wout[:, column(j)]), axis=0, keepdims=True)

    first = place[0] * depth
    for j in range(nj):
        row = readout[:, column(idx[j, first // BLK])]
        flat[...] = jnp.transpose(jnp.broadcast_to(row, (BLK, BLK)))
        pattern[:, block(j)] = flat[pl.ds(pl.multiple_of(first % BLK, depth), depth), :]
    pltpu.make_async_copy(upper, upper_out, sems.at[nf + 1]).wait()


def fixed_grads_kernel(orders, scale, nf, *refs):
    idx, place = refs[:2]
    ups, refs = refs[2 : 2 + nf], refs[2 + nf:]
    act_in, keep, send, ubuf, up, act, sems = refs
    rows = ubuf.shape[1]
    waits = [load(ups[d], ubuf.at[d], sems.at[d]) for d in range(nf)]
    act_wait = load(act_in, act, sems.at[nf])
    for d in range(nf):
        waits[d]()
        for b in range(up.shape[0]):
            up[b, d * rows : (d + 1) * rows, :] = ubuf[d, :, block(b)]
    act_wait()
    store_grads(idx, place, orders, scale, up, act, keep, send)


def backward_kernel(masks, orders, scale, nf, *refs):
    idx, place, here, left, right, teacher, turn, upper_in, dact_in, normed_in, act_in = refs[:11]
    parts, refs = refs[11 : 11 + len(masks)], refs[11 + len(masks):]
    own_coeff, along, keep, send = refs[:4]
    outs, refs = refs[4 : 4 + nf], refs[4 + nf:]
    upper, dact, normed, act, pre_grad, win, acc, sems = refs
    nj, kb = idx.shape
    rows = outs[0].shape[0]
    tokens = nf * rows
    nseg = teacher.shape[0]
    upper_wait = load(upper_in, upper, sems.at[0])
    dact_wait = load(dact_in, dact, sems.at[1])
    win_wait = load_weight(place, parts, masks, 0, win, sems.at[2])
    normed_wait = load(normed_in, normed, sems.at[3])
    act_wait = load(act_in, act, sems.at[4])
    acc[...] = jnp.zeros_like(acc)
    seg = (lax.broadcasted_iota(jnp.int32, (nseg, tokens), 0) + 1).astype(F32)
    sums = jnp.zeros((nseg, 1), F32)
    counts = jnp.zeros((nseg, 1), F32)
    for group in (here, left, right):
        member = group[:, tokens:] == seg
        sums = sums + jnp.sum(jnp.where(member, group[:, :tokens], 0.0), axis=1, keepdims=True)
        counts = counts + jnp.sum(jnp.where(member, 1.0, 0.0), axis=1, keepdims=True)
    misfit = sums / jnp.maximum(counts, 1.0) - teacher[...]
    coeff = 2.0 * LOSS_WEIGHT * jnp.sum(
        jnp.where(here[:, tokens:] == seg, misfit, 0.0), axis=0, keepdims=True
    )
    terms_of = three_terms(coeff * scale)
    across = jnp.transpose(jnp.broadcast_to(coeff, (BLK, tokens)))
    own_coeff[...] = across[:rows]
    upper_wait()
    dact_wait()
    win_wait()

    @loop(nj)
    def _(j):
        p = ((upper[j] + across * turn[:, column(j)]) * dact[j]).astype(BF16)
        pre_grad[j] = p
        terms = dot(p, win[:, column(j)], NT)
        for k in range(kb):
            acc[idx[j, k]] += terms[:, block(k)]

    spread(acc, outs, rows)
    normed_wait()
    store_grads(idx, place, orders, scale, normed, pre_grad, keep, send)
    act_wait()
    for j in range(nj):
        along[:, block(j)] = jnp.sum(dot(terms_of, act[j]), axis=0, keepdims=True)


def finish_kernel(x_ref, gain, upstream, readout, own_coeff, own, other, out):
    x = x_ref[...].astype(F32)
    inv = lax.rsqrt(jnp.mean(x * x, axis=1, keepdims=True) + EPS)
    g = (own[...] + other[...].astype(F32)) * gain[...]
    inner = jnp.mean(g * x, axis=1, keepdims=True)
    back = inv * g - x * (inv * inv * inv) * inner
    for b in range(x.shape[1] // BLK):
        cot = upstream[:, block(b)].astype(F32) + own_coeff[...] * readout[:, block(b)]
        out[:, block(b)] = (cot.astype(BF16).astype(F32) + back[:, block(b)]).astype(BF16)


VM = pl.BlockSpec(memory_space=pltpu.VMEM)
SM = pl.BlockSpec(memory_space=pltpu.SMEM)
HBM = pl.BlockSpec(memory_space=pltpu.HBM)


def call(body, outs, args, scratch, flops):
    return pl.pallas_call(
        body,
        out_shape=[pltpu.HBM(o.shape, o.dtype) if m is HBM else o for m, o in outs],
        in_specs=[m for m, _ in args],
        out_specs=[m for m, _ in outs],
        scratch_shapes=scratch,
        compiler_params=pltpu.CompilerParams(vmem_limit_bytes=VMEM_BYTES),
        cost_estimate=pl.CostEstimate(
            flops=flops,
            bytes_accessed=sum(math.prod(o.shape) * o.dtype.itemsize for _, o in outs),
            transcendentals=0,
        ),
    )(*[pltpu.with_memory_space_constraint(a, pltpu.HBM) if m is HBM else a for m, a in args])


def swap(value, axis, mask):
    n = lax.axis_size(axis)
    return lax.ppermute(value, axis, [(i, i ^ mask) for i in range(n)])


def swap_tok(value, even, odd):
    n = lax.axis_size("tok")
    return lax.ppermute(value, "tok", [(i, i ^ (odd if i & 1 else even)) for i in range(n)])


def after(value, *others):
    return lax.optimization_barrier((value, *others))[0]


def gather_tok(w_in, w_out, bits, ties):
    held, masks = [w_in, w_out], [[(0, 0)]]
    for step, (even, odd) in enumerate(zip(bits, bits[::-1])):
        whole = jnp.concatenate(held, axis=0)
        if step == len(bits) - 1:
            whole = after(whole, *ties[0])
        flat = [m for ms in masks for m in ms]
        held = [whole, swap_tok(whole, even, odd)]
        masks = [flat, [(a ^ even, b ^ odd) for a, b in flat]]
    other = [swap(after(h, *ties[1]), "tok", 1) for h in held]
    return held + other, masks + [[(b ^ 1, a ^ 1) for a, b in ms] for ms in masks]


def gather_feat(own, bits, far=None):
    held = {0: own}
    for bit in bits[::-1]:
        if bit == bits[-1] and far is not None:
            held[bit] = far
        else:
            held.update({
                m ^ bit: swap(held[m] if far is None else after(held[m], far), "feat", bit)
                for m in sorted(held)
            })
    return [held[d] for d in range(2 * bits[-1])]


def scatter_near(parts):
    held = {}
    for d in range(len(parts) - 2, 0, -2):
        held[d] = parts[d].astype(F32) + swap(parts[d + 1], "feat", 1).astype(F32)
    return held


def scatter_far(parts, held, bits, tie):
    firsts = [held[d] for d in sorted(held)]
    held = dict(held)
    held[0] = parts[0].astype(F32) + swap(after(parts[1], *firsts), "feat", 1).astype(F32)
    for bit in bits[1:]:
        stay = [d for d in held if not d & bit]
        for d in sorted(stay, reverse=True):
            got = swap(after(held[d | bit].astype(BF16), tie), "feat", bit)
            if d == 0 and bit == bits[-1]:
                return held[0], got
            held[d] = held[d] + got.astype(F32)
        held = {d: held[d] for d in stay}


def on_device(
    inputs, norm_gain, w_in, w_out, block_index, segment_ids, teacher_scores, upstream, readout
):
    rows, width = inputs.shape
    nt, nf = lax.axis_size("tok"), lax.axis_size("feat")
    nj, kb = block_index.shape
    hidden = w_in.shape[1]
    fb = width // BLK
    depth = w_in.shape[0]
    tokens = rows * nf
    grad_scale = 1.0 / math.sqrt(tokens * nt)
    bits = bits_of(nt)[1:]
    orders = (bits, bits[::-1])
    feat_bits = bits_of(nf)
    place = lax.axis_index("tok").astype(jnp.int32).reshape(1)
    gain_row, readout_row = norm_gain.reshape(1, width), readout.reshape(1, width)
    flops = 2 * tokens * hidden * kb * BLK
    sds = jax.ShapeDtypeStruct
    scalars = [(SM, block_index), (SM, place)]

    xs = gather_feat(inputs, feat_bits)
    near, far = xs[1], xs[feat_bits[-1]]
    upstream_far = swap(after(upstream, near, far), "feat", feat_bits[-1])
    ups = gather_feat(upstream, feat_bits, upstream_far)
    parts, masks = gather_tok(
        w_in, w_out, bits, ((near, far), xs[2:] + [upstream_far])
    )
    parts = [(HBM, p) for p in parts]

    by_feature = pltpu.VMEM((fb, tokens, BLK), BF16)
    by_hidden = pltpu.VMEM((nj, tokens, BLK), BF16)
    by_hidden_wide = pltpu.VMEM((nj, tokens, BLK), F32)
    weight = pltpu.VMEM((kb * BLK, hidden), BF16)
    summed = pltpu.VMEM((fb, tokens, BLK), F32)
    piece = sds((rows, width), BF16)
    half_grad = sds((kb * BLK // 2, hidden), BF16)

    outs = call(
        functools.partial(forward_kernel, masks, nf),
        [
            (HBM, sds((fb, tokens, BLK), BF16)),
            (HBM, sds((nj, tokens, BLK), BF16)),
            (HBM, sds((nj, tokens, BLK), F32)),
            (VM, sds((1, tokens + rows), F32)),
        ]
        + [(HBM, piece)] * nf,
        scalars
        + [(HBM, x) for x in xs]
        + [(VM, gain_row), (VM, readout_row), (VM, segment_ids.reshape(1, rows))]
        + parts,
        [
            pltpu.VMEM((nf, rows, width), BF16),
            by_feature,
            by_hidden,
            by_hidden_wide,
            weight,
            weight,
            summed,
            pltpu.VMEM((nf, rows, width), BF16),
            pltpu.SemaphoreType.DMA((nf + 5,)),
        ],
        2 * flops,
    )
    normed, act, dact, here = outs[:4]
    branch = outs[4:]

    upper, turn, pattern = call(
        functools.partial(upper_kernel, masks, nf),
        [
            (HBM, sds((nj, tokens, BLK), F32)),
            (VM, sds((1, hidden), F32)),
            (VM, sds((depth, hidden), F32)),
        ],
        scalars + [(HBM, u) for u in ups] + [(VM, readout_row)] + parts,
        [
            pltpu.VMEM((nf, rows, width), BF16),
            by_feature,
            weight,
            by_hidden_wide,
            pltpu.VMEM((BLK, BLK), F32),
            pltpu.SemaphoreType.DMA((nf + 2,)),
        ],
        flops,
    )
    keep_out, send_out = call(
        functools.partial(fixed_grads_kernel, orders, grad_scale, nf),
        [(VM, half_grad), (VM, half_grad)],
        scalars + [(HBM, u) for u in ups] + [(HBM, act)],
        [
            pltpu.VMEM((nf, rows, width), BF16),
            by_feature,
            by_hidden,
            pltpu.SemaphoreType.DMA((nf + 1,)),
        ],
        flops,
    )
    branch_near = scatter_near(branch)
    firsts = [branch_near[d] for d in sorted(branch_near)]
    for step, bit in enumerate(feat_bits):
        ties = ups[1:] if step == 0 else [keep_out, turn] + firsts
        there = swap(after(here, *ties), "feat", bit)
        turned = jnp.flip(there[:, :tokens].reshape(nf // (2 * bit), 2, bit * rows), axis=1)
        here = jnp.concatenate(
            [here[:, :tokens] + turned.reshape(1, tokens), here[:, tokens:], there[:, tokens:]],
            axis=1,
        )
    left = lax.ppermute(here, "tok", [(i, i + 1) for i in range(nt - 1)])
    right = lax.ppermute(here, "tok", [(i + 1, i) for i in range(nt - 1)])

    own, got = scatter_far(branch, branch_near, feat_bits, here)
    branch_sum = own + got.astype(F32)
    layer_out = (inputs.astype(F32) + branch_sum).astype(BF16)
    total_out = keep_out.astype(F32) + swap(send_out, "tok", 1).astype(F32)
    even, odd = bits[0], bits[-1]
    half = total_out.shape[0] // 2
    total_out = total_out[:half] + swap_tok(total_out[half:].astype(BF16), even, odd).astype(F32)

    outs = call(
        functools.partial(backward_kernel, masks, orders, grad_scale, nf),
        [
            (VM, sds((rows, BLK), F32)),
            (VM, sds((1, hidden), F32)),
            (VM, half_grad),
            (VM, half_grad),
        ]
        + [(VM, piece)] * nf,
        scalars
        + [(VM, here), (VM, left), (VM, right), (VM, teacher_scores.reshape(-1, 1)), (VM, turn)]
        + [(HBM, upper), (HBM, dact), (HBM, normed), (HBM, act)]
        + parts,
        [
            by_hidden_wide,
            by_hidden_wide,
            by_feature,
            by_hidden,
            by_hidden,
            weight,
            summed,
            pltpu.SemaphoreType.DMA((5,)),
        ],
        2 * flops,
    )
    own_coeff, along, keep_in, send_in = outs[:4]
    back = outs[4:]
    back_near = scatter_near(back)
    own, got = scatter_far(back, back_near, feat_bits, layer_out)

    send_in = after(send_in, layer_out, total_out)
    total = keep_in.astype(F32) + swap(send_in, "tok", 1).astype(F32)
    along = along + swap(along, "tok", 1)
    rest = list(zip(bits, bits[::-1]))
    for step, (even, odd) in enumerate(rest):
        half = total.shape[0] // 2
        away = after(total[half:].astype(BF16), along, total_out)
        along = along + swap_tok(after(along, total), even, odd)
        if step + 1 < len(rest):
            cut = total_out.shape[0] // 2
            got_out = swap_tok(after(total_out[cut:], total).astype(BF16), *rest[step + 1])
            total_out = total_out[:cut] + got_out.astype(F32)
        total = total[:half] + swap_tok(away, even, odd).astype(F32)
    grad_in = total
    grad_out = total_out + pattern * along
    (input_grad,) = call(
        finish_kernel,
        [(VM, piece)],
        [
            (VM, a)
            for a in (inputs, gain_row, upstream, readout_row, own_coeff, own, got)
        ],
        [],
        rows * width,
    )
    return (layer_out, input_grad, grad_in, grad_out)


def solution(mesh):
    return jax.shard_map(
        on_device,
        mesh=mesh,
        in_specs=(
            P(("tok", "feat"), None),
            P(),
            P("tok", "feat"),
            P("tok", "feat"),
            P("feat", None),
            P(("tok", "feat")),
            P(),
            P(("tok", "feat"), None),
            P(),
        ),
        out_specs=(
            P(("tok", "feat"), None),
            P(("tok", "feat"), None),
            P("tok", "feat"),
            P("tok", "feat"),
        ),
        check_vma=False,
    )
```

```python
import functools
import math

import jax
import jax.numpy as jnp
from jax import lax
from jax.experimental import pallas as pl
from jax.experimental.pallas import tpu as pltpu
from jax.sharding import PartitionSpec as P

BLK = 128
EPS = 1e-06
LOSS_WEIGHT = 8.0
GELU_A = math.sqrt(2.0 / math.pi)
GELU_B = 0.044715
VMEM_BYTES = 32 * 1024 * 1024
BF16 = jnp.bfloat16
F32 = jnp.float32
NN = (((1,), (0,)), ((), ()))
NT = (((1,), (1,)), ((), ()))
TN = (((0,), (0,)), ((), ()))


def dot(a, b, dims=NN):
    return lax.dot_general(a, b, dims, preferred_element_type=F32)


def block(b):
    return slice(b * BLK, (b + 1) * BLK)


def column(j):
    return pl.ds(pl.multiple_of(j * BLK, BLK), BLK)


def bits_of(n):
    return [1 << b for b in range(n.bit_length() - 1)]


def three_terms(row):
    hi = row.astype(BF16)
    rest = row - hi.astype(F32)
    mid = rest.astype(BF16)
    low = (rest - mid.astype(F32)).astype(BF16)
    pad = jnp.zeros((8 - 3, row.shape[1]), F32).astype(BF16)
    return jnp.concatenate([hi, mid, low, pad], axis=0)


def load_weight(place, parts, masks, which, whole, sem):
    core = place[0] & 1
    for part, ms in zip(parts, masks):
        depth = part.shape[0] // (2 * len(ms))
        for i, (even, odd) in enumerate(ms):
            owner = place[0] ^ jnp.where(core == 0, even, odd)
            at = pl.multiple_of(owner * depth, depth)
            pltpu.make_async_copy(
                part.at[pl.ds((2 * i + which) * depth, depth)], whole.at[pl.ds(at, depth)], sem
            ).start()
    return lambda: pltpu.make_async_copy(whole, whole, sem).wait()


def load(src, dst, sem):
    copy = pltpu.make_async_copy(src, dst, sem)
    copy.start()
    return copy.wait


def loop(nj, unroll=8):
    return pl.loop(0, nj, unroll=math.gcd(nj, unroll))


def spread(acc, outs, rows):
    for b in range(acc.shape[0]):
        part = acc[b].astype(BF16)
        for d, out in enumerate(outs):
            out[:, block(b)] = part[d * rows : (d + 1) * rows]


def forward_kernel(masks, nf, *refs):
    idx, place = refs[:2]
    xs, refs = refs[2 : 2 + nf], refs[2 + nf:]
    gain, readout, ids = refs[:3]
    parts, refs = refs[3 : 3 + len(masks)], refs[3 + len(masks):]
    normed_out, act_out, dact_out, score = refs[:4]
    branch_out, refs = refs[4 : 4 + nf], refs[4 + nf:]
    xbuf, normed, act, dact, win, wout, acc, branch, sems = refs
    rows = ids.shape[1]
    fb = normed.shape[0]
    nj, kb = idx.shape
    waits = [load(xs[d], xbuf.at[d], sems.at[d]) for d in range(nf)]
    win_wait = load_weight(place, parts, masks, 0, win, sems.at[nf])
    wout_wait = load_weight(place, parts, masks, 1, wout, sems.at[nf + 1])
    acc[...] = jnp.zeros_like(acc)
    own = jnp.zeros((8, rows), F32)
    for d in range(nf):
        waits[d]()
        x = xbuf[d].astype(F32)
        inv = lax.rsqrt(jnp.mean(x * x, axis=1, keepdims=True) + EPS)
        n = (x * inv * gain[...]).astype(BF16)
        for b in range(fb):
            normed[b, d * rows : (d + 1) * rows, :] = n[:, block(b)]
            if d == 0:
                own = own + dot(three_terms(readout[:, block(b)]), xbuf[0, :, block(b)], NT)
    normed_wait = load(normed, normed_out, sems.at[nf + 2])
    win_wait()
    wout_wait()

    @loop(nj)
    def _(j):
        which = [idx[j, k] for k in range(kb)]
        picked = jnp.concatenate([normed[w] for w in which], axis=1)
        v = dot(picked, win[:, column(j)])
        v2 = v * v
        t = jnp.tanh(GELU_A * v * (1.0 + GELU_B * v2))
        half = 0.5 * (1.0 + t)
        a = (v * half).astype(BF16)
        act[j] = a
        dact[j] = half + 0.5 * v * (1.0 - t * t) * (GELU_A * (1.0 + 3.0 * GELU_B * v2))
        pltpu.make_async_copy(act.at[j], act_out.at[j], sems.at[nf + 3]).start()
        pltpu.make_async_copy(dact.at[j], dact_out.at[j], sems.at[nf + 4]).start()
        terms = dot(a, wout[:, column(j)], NT)
        for k, w in enumerate(which):
            acc[w] += terms[:, block(k)]

    act_wait = pltpu.make_async_copy(act, act_out, sems.at[nf + 3]).wait
    dact_wait = pltpu.make_async_copy(dact, dact_out, sems.at[nf + 4]).wait
    spread(acc, [branch.at[d] for d in range(nf)], rows)
    waits = [load(branch.at[d], branch_out[d], sems.at[d]) for d in range(nf)]
    total = jnp.zeros((8, nf * rows), F32)
    for b in range(fb):
        total = total + dot(three_terms(readout[:, block(b)]), acc[b].astype(BF16), NT)
    own = jnp.sum(own, axis=0, keepdims=True)
    pad = jnp.zeros((1, (nf - 1) * rows), F32)
    row = jnp.sum(total, axis=0, keepdims=True) + jnp.concatenate([own, pad], axis=1)
    score[...] = jnp.concatenate([row, ids[...].astype(F32) + 1.0], axis=1)
    for wait in waits + [normed_wait, act_wait, dact_wait]:
        wait()


def store_grads(idx, place, orders, scale, pairs, keep, send):
    nj, kb = idx.shape
    count = 2 << len(orders[0])
    depth = kb * BLK // count
    per = BLK // depth
    core = place[0] & 1

    def slot(owner, order):
        m = place[0] ^ owner
        pos = 0
        for bit in order:
            pos = 2 * pos + jnp.where((m & bit) != 0, 1, 0)
        return pos * len(pairs) * depth

    def slots(own):
        return [
            jnp.where(own == 0, slot(2 * q, orders[0]), slot(2 * q, orders[1]))
            for q in range(count // 2)
        ]

    keep_at, send_at = slots(core), slots(1 - core)

    @loop(nj, 4)
    def _(j):
        for which, (left, right) in enumerate(pairs):
            for k in range(kb):
                g = (dot(left[idx[j, k]], right[j], TN) * scale).astype(BF16)
                for half in range(per // 2):
                    q = k * (per // 2) + half
                    even = g[2 * half * depth : (2 * half + 1) * depth]
                    odd = g[(2 * half + 1) * depth : (2 * half + 2) * depth]
                    kept = pl.multiple_of(keep_at[q] + which * depth, depth)
                    sent = pl.multiple_of(send_at[q] + which * depth, depth)
                    keep[pl.ds(kept, depth), column(j)] = jnp.where(core == 0, even, odd)
                    send[pl.ds(sent, depth), column(j)] = jnp.where(core == 0, odd, even)


def upper_kernel(masks, nf, *refs):
    idx, place = refs[:2]
    ups, refs = refs[2 : 2 + nf], refs[2 + nf:]
    readout, refs = refs[0], refs[1:]
    parts, refs = refs[: len(masks)], refs[len(masks):]
    upper_out, turn, ubuf, up, wout, upper, sems = refs
    nj, kb = idx.shape
    fb = up.shape[0]
    rows = ubuf.shape[1]
    waits = [load(ups[d], ubuf.at[d], sems.at[d]) for d in range(nf)]
    wout_wait = load_weight(place, parts, masks, 1, wout, sems.at[nf])
    for d in range(nf):
        waits[d]()
        for b in range(fb):
            up[b, d * rows : (d + 1) * rows, :] = ubuf[d, :, block(b)]
    wout_wait()

    @loop(nj)
    def _(j):
        which = [idx[j, k] for k in range(kb)]
        picked = jnp.concatenate([up[w] for w in which], axis=1)
        turned = jnp.concatenate([three_terms(readout[:, column(w)]) for w in which], axis=1)
        rows_of = jnp.concatenate([picked, turned, jnp.zeros_like(turned)], axis=0)
        both = dot(rows_of, wout[:, column(j)])
        upper[j] = both[: nf * rows]
        pltpu.make_async_copy(upper.at[j], upper_out.at[j], sems.at[nf + 1]).start()
        turn[:, column(j)] = jnp.sum(both[nf * rows : nf * rows + 8], axis=0, keepdims=True)

    pltpu.make_async_copy(upper, upper_out, sems.at[nf + 1]).wait()


def grads_kernel(orders, scale, nf, *refs):
    idx, place, here, left, right, teacher, turn, readout, upper_in, dact_in, normed_in, act_in = refs[:12]
    ups, refs = refs[12 : 12 + nf], refs[12 + nf:]
    own_coeff, pre_grad, keep, send, upper, dact, normed, act, cot, ubuf, sems = refs
    nj, kb = idx.shape
    rows = ubuf.shape[1]
    tokens = nf * rows
    nseg = teacher.shape[0]
    up_waits = [load(ups[d], ubuf.at[d], sems.at[4 + d]) for d in range(nf)]
    upper_wait = load(upper_in, upper, sems.at[0])
    dact_wait = load(dact_in, dact, sems.at[1])
    normed_wait = load(normed_in, normed, sems.at[2])
    act_wait = load(act_in, act, sems.at[3])
    seg = (lax.broadcasted_iota(jnp.int32, (nseg, tokens), 0) + 1).astype(F32)
    sums = jnp.zeros((nseg, 1), F32)
    counts = jnp.zeros((nseg, 1), F32)
    for group in (here, left, right):
        member = group[:, tokens:] == seg
        sums = sums + jnp.sum(jnp.where(member, group[:, :tokens], 0.0), axis=1, keepdims=True)
        counts = counts + jnp.sum(jnp.where(member, 1.0, 0.0), axis=1, keepdims=True)
    misfit = sums / jnp.maximum(counts, 1.0) - teacher[...]
    coeff = 2.0 * LOSS_WEIGHT * jnp.sum(
        jnp.where(here[:, tokens:] == seg, misfit, 0.0), axis=0, keepdims=True
    )
    across = jnp.transpose(jnp.broadcast_to(coeff, (BLK, tokens)))
    own_coeff[...] = across[:rows]
    for d in range(nf):
        up_waits[d]()
        part = across[d * rows : (d + 1) * rows]
        for b in range(cot.shape[0]):
            c = ubuf[d, :, block(b)].astype(F32) + part * readout[:, block(b)]
            cot[b, d * rows : (d + 1) * rows, :] = c.astype(BF16)
    upper_wait()
    dact_wait()

    @loop(nj)
    def _(j):
        pre_grad[j] = ((upper[j] + across * turn[:, column(j)]) * dact[j]).astype(BF16)

    normed_wait()
    act_wait()
    store_grads(idx, place, orders, scale, ((cot, act), (normed, pre_grad)), keep, send)


def back_kernel(masks, nf, *refs):
    idx, place, pre_grad = refs[:3]
    parts, refs = refs[3 : 3 + len(masks)], refs[3 + len(masks):]
    outs, (win, acc, sem) = refs[:nf], refs[nf:]
    nj, kb = idx.shape
    win_wait = load_weight(place, parts, masks, 0, win, sem)
    acc[...] = jnp.zeros_like(acc)
    win_wait()

    @loop(nj)
    def _(j):
        terms = dot(pre_grad[j], win[:, column(j)], NT)
        for k in range(kb):
            acc[idx[j, k]] += terms[:, block(k)]

    spread(acc, outs, outs[0].shape[0])


def finish_kernel(x_ref, gain, upstream, readout, own_coeff, own, other, out):
    x = x_ref[...].astype(F32)
    inv = lax.rsqrt(jnp.mean(x * x, axis=1, keepdims=True) + EPS)
    g = (own[...] + other[...].astype(F32)) * gain[...]
    inner = jnp.mean(g * x, axis=1, keepdims=True)
    back = inv * g - x * (inv * inv * inv) * inner
    for b in range(x.shape[1] // BLK):
        cot = upstream[:, block(b)].astype(F32) + own_coeff[...] * readout[:, block(b)]
        out[:, block(b)] = (cot.astype(BF16).astype(F32) + back[:, block(b)]).astype(BF16)


VM = pl.BlockSpec(memory_space=pltpu.VMEM)
SM = pl.BlockSpec(memory_space=pltpu.SMEM)
HBM = pl.BlockSpec(memory_space=pltpu.HBM)


def call(body, outs, args, scratch, flops):
    return pl.pallas_call(
        body,
        out_shape=[pltpu.HBM(o.shape, o.dtype) if m is HBM else o for m, o in outs],
        in_specs=[m for m, _ in args],
        out_specs=[m for m, _ in outs],
        scratch_shapes=scratch,
        compiler_params=pltpu.CompilerParams(vmem_limit_bytes=VMEM_BYTES),
        cost_estimate=pl.CostEstimate(
            flops=flops,
            bytes_accessed=sum(math.prod(o.shape) * o.dtype.itemsize for _, o in outs),
            transcendentals=0,
        ),
    )(*[pltpu.with_memory_space_constraint(a, pltpu.HBM) if m is HBM else a for m, a in args])


def swap(value, axis, mask):
    n = lax.axis_size(axis)
    return lax.ppermute(value, axis, [(i, i ^ mask) for i in range(n)])


def swap_tok(value, even, odd):
    n = lax.axis_size("tok")
    return lax.ppermute(value, "tok", [(i, i ^ (odd if i & 1 else even)) for i in range(n)])


def after(value, *others):
    return lax.optimization_barrier((value, *others))[0]


def gather_tok(w_in, w_out, bits, ties):
    held, masks = [w_in, w_out], [[(0, 0)]]
    for step, (even, odd) in enumerate(zip(bits, bits[::-1])):
        whole = jnp.concatenate(held, axis=0)
        if step == len(bits) - 1:
            whole = after(whole, *ties[0])
        flat = [m for ms in masks for m in ms]
        held = [whole, swap_tok(whole, even, odd)]
        masks = [flat, [(a ^ even, b ^ odd) for a, b in flat]]
    other = [swap(after(h, *ties[1]), "tok", 1) for h in held]
    return held + other, masks + [[(b ^ 1, a ^ 1) for a, b in ms] for ms in masks]


class Halving:
    def __init__(self, terms):
        self.terms = terms

    def total(self):
        return functools.reduce(lambda a, b: a + b, [t.astype(F32) for t in self.terms])

    def away(self):
        half = self.terms[0].shape[0] // 2
        sent = Halving([t[half:] for t in self.terms]).total().astype(BF16)
        self.terms = [t[:half] for t in self.terms]
        return sent

    def add(self, term):
        self.terms.append(term)


def gather_feat(own, bits, far=None):
    held = {0: own}
    for bit in bits[::-1]:
        if bit == bits[-1] and far is not None:
            held[bit] = far
        else:
            held.update({
                m ^ bit: swap(held[m] if far is None else after(held[m], far), "feat", bit)
                for m in sorted(held)
            })
    return [held[d] for d in range(2 * bits[-1])]


def scatter_near(parts):
    return {d: swap(parts[d + 1], "feat", 1) for d in range(len(parts) - 2, 0, -2)}


def scatter_far(parts, held, bits, tie):
    firsts = [held[d] for d in sorted(held)]
    held = {d: parts[d].astype(F32) + got.astype(F32) for d, got in held.items()}
    beside = swap(after(parts[1], *firsts), "feat", 1)
    held[0] = parts[0].astype(F32) + beside.astype(F32)
    for bit in bits[1:]:
        stay = [d for d in held if not d & bit]
        for d in sorted(stay, reverse=True):
            got = swap(after(held[d | bit].astype(BF16), tie), "feat", bit)
            if d == 0 and bit == bits[-1]:
                return held[0], got, beside
            held[d] = held[d] + got.astype(F32)
        held = {d: held[d] for d in stay}


def on_device(
    inputs, norm_gain, w_in, w_out, block_index, segment_ids, teacher_scores, upstream, readout
):
    rows, width = inputs.shape
    nt, nf = lax.axis_size("tok"), lax.axis_size("feat")
    nj, kb = block_index.shape
    hidden = w_in.shape[1]
    fb = width // BLK
    depth = w_in.shape[0]
    tokens = rows * nf
    grad_scale = 1.0 / math.sqrt(tokens * nt)
    bits = bits_of(nt)[1:]
    orders = (bits, bits[::-1])
    feat_bits = bits_of(nf)
    place = lax.axis_index("tok").astype(jnp.int32).reshape(1)
    gain_row, readout_row = norm_gain.reshape(1, width), readout.reshape(1, width)
    flops = 2 * tokens * hidden * kb * BLK
    sds = jax.ShapeDtypeStruct
    scalars = [(SM, block_index), (SM, place)]

    xs = gather_feat(inputs, feat_bits)
    near, far = xs[1], xs[feat_bits[-1]]
    upstream_far = swap(after(upstream, near, far), "feat", feat_bits[-1])
    ups = gather_feat(upstream, feat_bits, upstream_far)
    parts, masks = gather_tok(
        w_in, w_out, bits, ((near, far), xs[2:] + [upstream_far])
    )
    parts = [(HBM, p) for p in parts]

    by_feature = pltpu.VMEM((fb, tokens, BLK), BF16)
    by_hidden = pltpu.VMEM((nj, tokens, BLK), BF16)
    by_hidden_wide = pltpu.VMEM((nj, tokens, BLK), F32)
    weight = pltpu.VMEM((kb * BLK, hidden), BF16)
    summed = pltpu.VMEM((fb, tokens, BLK), F32)
    piece = sds((rows, width), BF16)

    outs = call(
        functools.partial(forward_kernel, masks, nf),
        [
            (HBM, sds((fb, tokens, BLK), BF16)),
            (HBM, sds((nj, tokens, BLK), BF16)),
            (HBM, sds((nj, tokens, BLK), F32)),
            (VM, sds((1, tokens + rows), F32)),
        ]
        + [(HBM, piece)] * nf,
        scalars
        + [(HBM, x) for x in xs]
        + [(VM, gain_row), (VM, readout_row), (VM, segment_ids.reshape(1, rows))]
        + parts,
        [
            pltpu.VMEM((nf, rows, width), BF16),
            by_feature,
            by_hidden,
            by_hidden_wide,
            weight,
            weight,
            summed,
            pltpu.VMEM((nf, rows, width), BF16),
            pltpu.SemaphoreType.DMA((nf + 5,)),
        ],
        2 * flops,
    )
    normed, act, dact, here = outs[:4]
    branch = outs[4:]

    upper, turn = call(
        functools.partial(upper_kernel, masks, nf),
        [
            (HBM, sds((nj, tokens, BLK), F32)),
            (VM, sds((1, hidden), F32)),
        ],
        scalars + [(HBM, u) for u in ups] + [(VM, readout_row)] + parts,
        [
            pltpu.VMEM((nf, rows, width), BF16),
            by_feature,
            weight,
            by_hidden_wide,
            pltpu.SemaphoreType.DMA((nf + 2,)),
        ],
        flops,
    )
    for step, bit in enumerate(feat_bits):
        there = swap(after(here, *ups[1:]) if step == 0 else here, "feat", bit)
        if step == 0:
            branch_near = scatter_near([after(b, there) for b in branch])
        if bit == feat_bits[-1]:
            there = after(there, turn)
        turned = jnp.flip(there[:, :tokens].reshape(nf // (2 * bit), 2, bit * rows), axis=1)
        here = jnp.concatenate(
            [here[:, :tokens] + turned.reshape(1, tokens), here[:, tokens:], there[:, tokens:]],
            axis=1,
        )
    left = swap(here, "tok", 1)
    odd = range(1, nt - 1, 2)
    right = lax.ppermute(here, "tok", [(i, i + 1) for i in odd] + [(i + 1, i) for i in odd])

    branch_near = {d: after(got, turn) for d, got in branch_near.items()}
    half_grads = sds((kb * BLK, hidden), BF16)
    own_coeff, pre_grad, keep, send = call(
        functools.partial(grads_kernel, orders, grad_scale, nf),
        [
            (VM, sds((rows, BLK), F32)),
            (VM, sds((nj, tokens, BLK), BF16)),
            (VM, half_grads),
            (VM, half_grads),
        ],
        scalars
        + [(VM, here), (VM, left), (VM, right), (VM, teacher_scores.reshape(-1, 1)), (VM, turn)]
        + [(VM, readout_row)]
        + [(HBM, a) for a in (upper, dact, normed, act)]
        + [(HBM, u) for u in ups],
        [
            by_hidden_wide,
            by_hidden_wide,
            by_feature,
            by_hidden,
            by_feature,
            pltpu.VMEM((nf, rows, width), BF16),
            pltpu.SemaphoreType.DMA((nf + 4,)),
        ],
        2 * flops,
    )
    back = call(
        functools.partial(back_kernel, masks, nf),
        [(VM, piece)] * nf,
        scalars + [(VM, pre_grad)] + parts,
        [weight, summed, pltpu.SemaphoreType.DMA],
        flops,
    )
    branch_own, branch_got, beside = scatter_far(branch, branch_near, feat_bits, here)
    branch_got = after(branch_got, own_coeff)
    layer_out = (inputs.astype(F32) + (branch_own + branch_got.astype(F32))).astype(BF16)
    send = after(send, branch_got, beside)
    own, got, _ = scatter_far(back, scatter_near(back), feat_bits, branch_got)
    sums = Halving([keep, after(swap(send, "tok", 1), back[1])])
    for pair in zip(bits, bits[::-1]):
        sums.add(swap_tok(sums.away(), *pair))
    grads = sums.total()
    grad_out, grad_in = grads[:depth], grads[depth:]
    (input_grad,) = call(
        finish_kernel,
        [(VM, piece)],
        [
            (VM, a)
            for a in (inputs, gain_row, upstream, readout_row, own_coeff, own, got)
        ],
        [],
        rows * width,
    )
    return (layer_out, input_grad, grad_in, grad_out)


def solution(mesh):
    return jax.shard_map(
        on_device,
        mesh=mesh,
        in_specs=(
            P(("tok", "feat"), None),
            P(),
            P("tok", "feat"),
            P("tok", "feat"),
            P("feat", None),
            P(("tok", "feat")),
            P(),
            P(("tok", "feat"), None),
            P(),
        ),
        out_specs=(
            P(("tok", "feat"), None),
            P(("tok", "feat"), None),
            P("tok", "feat"),
            P("tok", "feat"),
        ),
        check_vma=False,
    )
```

```python
import functools
import math

import jax
import jax.numpy as jnp
from jax import lax
from jax.experimental import pallas as pl
from jax.experimental.pallas import tpu as pltpu
from jax.sharding import PartitionSpec as P

BLK = 128
EPS = 1e-06
LOSS_WEIGHT = 8.0
GELU_A = math.sqrt(2.0 / math.pi)
GELU_B = 0.044715
VMEM_BYTES = 32 * 1024 * 1024
BF16 = jnp.bfloat16
F32 = jnp.float32
NN = (((1,), (0,)), ((), ()))
NT = (((1,), (1,)), ((), ()))
TN = (((0,), (0,)), ((), ()))


def dot(a, b, dims=NN):
    return lax.dot_general(a, b, dims, preferred_element_type=F32)


def block(b):
    return slice(b * BLK, (b + 1) * BLK)


def column(j):
    return pl.ds(pl.multiple_of(j * BLK, BLK), BLK)


def bits_of(n):
    return [1 << b for b in range(n.bit_length() - 1)]


def three_terms(row):
    hi = row.astype(BF16)
    rest = row - hi.astype(F32)
    mid = rest.astype(BF16)
    low = (rest - mid.astype(F32)).astype(BF16)
    pad = jnp.zeros((8 - 3, row.shape[1]), F32).astype(BF16)
    return jnp.concatenate([hi, mid, low, pad], axis=0)


def load_weight(place, parts, masks, which, whole, sem):
    core = place[0] & 1
    for part, ms in zip(parts, masks):
        depth = part.shape[0] // (2 * len(ms))
        for i, (even, odd) in enumerate(ms):
            owner = place[0] ^ jnp.where(core == 0, even, odd)
            at = pl.multiple_of(owner * depth, depth)
            pltpu.make_async_copy(
                part.at[pl.ds((2 * i + which) * depth, depth)], whole.at[pl.ds(at, depth)], sem
            ).start()
    return lambda: pltpu.make_async_copy(whole, whole, sem).wait()


def load(src, dst, sem):
    copy = pltpu.make_async_copy(src, dst, sem)
    copy.start()
    return copy.wait


def loop(nj, unroll=8):
    return pl.loop(0, nj, unroll=math.gcd(nj, unroll))


def spread(acc, outs, rows):
    for b in range(acc.shape[0]):
        part = acc[b].astype(BF16)
        for d, out in enumerate(outs):
            out[:, block(b)] = part[d * rows : (d + 1) * rows]


def forward_kernel(masks, nf, *refs):
    idx, place = refs[:2]
    xs, refs = refs[2 : 2 + nf], refs[2 + nf:]
    gain, readout, ids = refs[:3]
    parts, refs = refs[3 : 3 + len(masks)], refs[3 + len(masks):]
    normed_out, act_out, dact_out, score = refs[:4]
    branch_out, refs = refs[4 : 4 + nf], refs[4 + nf:]
    xbuf, normed, act, dact, win, wout, acc, branch, sems = refs
    rows = ids.shape[1]
    fb = normed.shape[0]
    nj, kb = idx.shape
    waits = [load(xs[d], xbuf.at[d], sems.at[d]) for d in range(nf)]
    win_wait = load_weight(place, parts, masks, 0, win, sems.at[nf])
    wout_wait = load_weight(place, parts, masks, 1, wout, sems.at[nf + 1])
    acc[...] = jnp.zeros_like(acc)
    own = jnp.zeros((8, rows), F32)
    for d in range(nf):
        waits[d]()
        x = xbuf[d].astype(F32)
        inv = lax.rsqrt(jnp.mean(x * x, axis=1, keepdims=True) + EPS)
        n = (x * inv * gain[...]).astype(BF16)
        for b in range(fb):
            normed[b, d * rows : (d + 1) * rows, :] = n[:, block(b)]
            if d == 0:
                own = own + dot(three_terms(readout[:, block(b)]), xbuf[0, :, block(b)], NT)
    normed_wait = load(normed, normed_out, sems.at[nf + 2])
    win_wait()
    wout_wait()

    @loop(nj)
    def _(j):
        which = [idx[j, k] for k in range(kb)]
        picked = jnp.concatenate([normed[w] for w in which], axis=1)
        v = dot(picked, win[:, column(j)])
        v2 = v * v
        t = jnp.tanh(GELU_A * v * (1.0 + GELU_B * v2))
        half = 0.5 * (1.0 + t)
        a = (v * half).astype(BF16)
        act[j] = a
        slope = half + 0.5 * v * (1.0 - t * t) * (GELU_A * (1.0 + 3.0 * GELU_B * v2))
        dact[j] = slope.astype(BF16)
        pltpu.make_async_copy(act.at[j], act_out.at[j], sems.at[nf + 3]).start()
        pltpu.make_async_copy(dact.at[j], dact_out.at[j], sems.at[nf + 4]).start()
        terms = dot(a, wout[:, column(j)], NT)
        for k, w in enumerate(which):
            acc[w] += terms[:, block(k)]

    act_wait = pltpu.make_async_copy(act, act_out, sems.at[nf + 3]).wait
    dact_wait = pltpu.make_async_copy(dact, dact_out, sems.at[nf + 4]).wait
    spread(acc, [branch.at[d] for d in range(nf)], rows)
    waits = [load(branch.at[d], branch_out[d], sems.at[d]) for d in range(nf)]
    total = jnp.zeros((8, nf * rows), F32)
    for b in range(fb):
        total = total + dot(three_terms(readout[:, block(b)]), acc[b].astype(BF16), NT)
    own = jnp.sum(own, axis=0, keepdims=True)
    pad = jnp.zeros((1, (nf - 1) * rows), F32)
    row = jnp.sum(total, axis=0, keepdims=True) + jnp.concatenate([own, pad], axis=1)
    score[...] = jnp.concatenate([row, ids[...].astype(F32) + 1.0], axis=1)
    for wait in waits + [normed_wait, act_wait, dact_wait]:
        wait()


def store_grads(idx, place, orders, scale, pairs, keep, send):
    nj, kb = idx.shape
    count = 2 << len(orders[0])
    depth = kb * BLK // count
    per = BLK // depth
    core = place[0] & 1

    def slot(owner, order):
        m = place[0] ^ owner
        pos = 0
        for bit in order:
            pos = 2 * pos + jnp.where((m & bit) != 0, 1, 0)
        return pos * len(pairs) * depth

    def slots(own):
        return [
            jnp.where(own == 0, slot(2 * q, orders[0]), slot(2 * q, orders[1]))
            for q in range(count // 2)
        ]

    keep_at, send_at = slots(core), slots(1 - core)

    @loop(nj, 4)
    def _(j):
        for which, (left, right) in enumerate(pairs):
            for k in range(kb):
                g = (dot(left[idx[j, k]], right[j], TN) * scale).astype(BF16)
                for half in range(per // 2):
                    q = k * (per // 2) + half
                    even = g[2 * half * depth : (2 * half + 1) * depth]
                    odd = g[(2 * half + 1) * depth : (2 * half + 2) * depth]
                    kept = pl.multiple_of(keep_at[q] + which * depth, depth)
                    sent = pl.multiple_of(send_at[q] + which * depth, depth)
                    keep[pl.ds(kept, depth), column(j)] = jnp.where(core == 0, even, odd)
                    send[pl.ds(sent, depth), column(j)] = jnp.where(core == 0, odd, even)


def upper_kernel(masks, nf, *refs):
    idx, place = refs[:2]
    ups, refs = refs[2 : 2 + nf], refs[2 + nf:]
    readout, refs = refs[0], refs[1:]
    parts, refs = refs[: len(masks)], refs[len(masks):]
    upper_out, turn, ubuf, up, wout, upper, sems = refs
    nj, kb = idx.shape
    fb = up.shape[0]
    rows = ubuf.shape[1]
    waits = [load(ups[d], ubuf.at[d], sems.at[d]) for d in range(nf)]
    wout_wait = load_weight(place, parts, masks, 1, wout, sems.at[nf])
    for d in range(nf):
        waits[d]()
        for b in range(fb):
            up[b, d * rows : (d + 1) * rows, :] = ubuf[d, :, block(b)]
    wout_wait()

    @loop(nj)
    def _(j):
        which = [idx[j, k] for k in range(kb)]
        picked = jnp.concatenate([up[w] for w in which], axis=1)
        turned = jnp.concatenate([three_terms(readout[:, column(w)]) for w in which], axis=1)
        rows_of = jnp.concatenate([picked, turned, jnp.zeros_like(turned)], axis=0)
        both = dot(rows_of, wout[:, column(j)])
        upper[j] = both[: nf * rows].astype(BF16)
        pltpu.make_async_copy(upper.at[j], upper_out.at[j], sems.at[nf + 1]).start()
        turn[:, column(j)] = jnp.sum(both[nf * rows : nf * rows + 8], axis=0, keepdims=True)

    pltpu.make_async_copy(upper, upper_out, sems.at[nf + 1]).wait()


def grads_kernel(orders, scale, nf, *refs):
    idx, place, here, left, right, teacher, turn, readout, upper_in, dact_in, normed_in, act_in = refs[:12]
    ups, refs = refs[12 : 12 + nf], refs[12 + nf:]
    own_coeff, pre_grad, keep, send, upper, dact, normed, act, cot, ubuf, sems = refs
    nj, kb = idx.shape
    rows = ubuf.shape[1]
    tokens = nf * rows
    nseg = teacher.shape[0]
    up_waits = [load(ups[d], ubuf.at[d], sems.at[4 + d]) for d in range(nf)]
    upper_wait = load(upper_in, upper, sems.at[0])
    dact_wait = load(dact_in, dact, sems.at[1])
    normed_wait = load(normed_in, normed, sems.at[2])
    act_wait = load(act_in, act, sems.at[3])
    seg = (lax.broadcasted_iota(jnp.int32, (nseg, tokens), 0) + 1).astype(F32)
    sums = jnp.zeros((nseg, 1), F32)
    counts = jnp.zeros((nseg, 1), F32)
    for group in (here, left, right):
        member = group[:, tokens:] == seg
        sums = sums + jnp.sum(jnp.where(member, group[:, :tokens], 0.0), axis=1, keepdims=True)
        counts = counts + jnp.sum(jnp.where(member, 1.0, 0.0), axis=1, keepdims=True)
    misfit = sums / jnp.maximum(counts, 1.0) - teacher[...]
    coeff = 2.0 * LOSS_WEIGHT * jnp.sum(
        jnp.where(here[:, tokens:] == seg, misfit, 0.0), axis=0, keepdims=True
    )
    across = jnp.transpose(jnp.broadcast_to(coeff, (BLK, tokens)))
    own_coeff[...] = across[:rows]
    for d in range(nf):
        up_waits[d]()
        part = across[d * rows : (d + 1) * rows]
        for b in range(cot.shape[0]):
            c = ubuf[d, :, block(b)].astype(F32) + part * readout[:, block(b)]
            cot[b, d * rows : (d + 1) * rows, :] = c.astype(BF16)
    upper_wait()
    dact_wait()

    @loop(nj)
    def _(j):
        whole = upper[j].astype(F32) + across * turn[:, column(j)]
        pre_grad[j] = (whole * dact[j].astype(F32)).astype(BF16)

    normed_wait()
    act_wait()
    store_grads(idx, place, orders, scale, ((cot, act), (normed, pre_grad)), keep, send)


def back_kernel(masks, nf, *refs):
    idx, place, pre_grad = refs[:3]
    parts, refs = refs[3 : 3 + len(masks)], refs[3 + len(masks):]
    outs, (win, acc, sem) = refs[:nf], refs[nf:]
    nj, kb = idx.shape
    win_wait = load_weight(place, parts, masks, 0, win, sem)
    acc[...] = jnp.zeros_like(acc)
    win_wait()

    @loop(nj)
    def _(j):
        terms = dot(pre_grad[j], win[:, column(j)], NT)
        for k in range(kb):
            acc[idx[j, k]] += terms[:, block(k)]

    spread(acc, outs, outs[0].shape[0])


def finish_kernel(x_ref, gain, upstream, readout, own_coeff, own, other, out):
    x = x_ref[...].astype(F32)
    inv = lax.rsqrt(jnp.mean(x * x, axis=1, keepdims=True) + EPS)
    g = (own[...] + other[...].astype(F32)) * gain[...]
    inner = jnp.mean(g * x, axis=1, keepdims=True)
    back = inv * g - x * (inv * inv * inv) * inner
    for b in range(x.shape[1] // BLK):
        cot = upstream[:, block(b)].astype(F32) + own_coeff[...] * readout[:, block(b)]
        out[:, block(b)] = (cot.astype(BF16).astype(F32) + back[:, block(b)]).astype(BF16)


VM = pl.BlockSpec(memory_space=pltpu.VMEM)
SM = pl.BlockSpec(memory_space=pltpu.SMEM)
HBM = pl.BlockSpec(memory_space=pltpu.HBM)


def call(body, outs, args, scratch, flops):
    return pl.pallas_call(
        body,
        out_shape=[pltpu.HBM(o.shape, o.dtype) if m is HBM else o for m, o in outs],
        in_specs=[m for m, _ in args],
        out_specs=[m for m, _ in outs],
        scratch_shapes=scratch,
        compiler_params=pltpu.CompilerParams(vmem_limit_bytes=VMEM_BYTES),
        cost_estimate=pl.CostEstimate(
            flops=flops,
            bytes_accessed=sum(math.prod(o.shape) * o.dtype.itemsize for _, o in outs),
            transcendentals=0,
        ),
    )(*[pltpu.with_memory_space_constraint(a, pltpu.HBM) if m is HBM else a for m, a in args])


def swap(value, axis, mask):
    n = lax.axis_size(axis)
    return lax.ppermute(value, axis, [(i, i ^ mask) for i in range(n)])


def swap_tok(value, even, odd):
    n = lax.axis_size("tok")
    return lax.ppermute(value, "tok", [(i, i ^ (odd if i & 1 else even)) for i in range(n)])


def after(value, *others):
    return lax.optimization_barrier((value, *others))[0]


def gather_tok(w_in, w_out, bits, ties):
    held, masks = [w_in, w_out], [[(0, 0)]]
    for step, (even, odd) in enumerate(zip(bits, bits[::-1])):
        whole = jnp.concatenate(held, axis=0)
        if step == len(bits) - 1:
            whole = after(whole, *ties[0])
        flat = [m for ms in masks for m in ms]
        held = [whole, swap_tok(whole, even, odd)]
        masks = [flat, [(a ^ even, b ^ odd) for a, b in flat]]
    other = [swap(after(h, *tie), "tok", 1) for h, tie in zip(held, ties[1:])]
    return held + other, masks + [[(b ^ 1, a ^ 1) for a, b in ms] for ms in masks]


class Halving:
    def __init__(self, terms):
        self.terms = terms

    def total(self):
        return functools.reduce(lambda a, b: a + b, [t.astype(F32) for t in self.terms])

    def away(self):
        half = self.terms[0].shape[0] // 2
        sent = Halving([t[half:] for t in self.terms]).total().astype(BF16)
        self.terms = [t[:half] for t in self.terms]
        return sent

    def add(self, term):
        self.terms.append(term)


def gather_feat(own, bits, far=None):
    held = {0: own}
    for bit in bits[::-1]:
        if bit == bits[-1] and far is not None:
            held[bit] = far
        else:
            held.update({
                m ^ bit: swap(held[m] if far is None else after(held[m], far), "feat", bit)
                for m in sorted(held)
            })
    return [held[d] for d in range(2 * bits[-1])]


def scatter_near(parts):
    return {d: swap(parts[d + 1], "feat", 1) for d in range(len(parts) - 2, 0, -2)}


def scatter_far(parts, held, bits, tie):
    firsts = [held[d] for d in sorted(held)]
    held = {d: parts[d].astype(F32) + got.astype(F32) for d, got in held.items()}
    beside = swap(after(parts[1], *firsts), "feat", 1)
    held[0] = parts[0].astype(F32) + beside.astype(F32)
    for bit in bits[1:]:
        stay = [d for d in held if not d & bit]
        for d in sorted(stay, reverse=True):
            got = swap(after(held[d | bit].astype(BF16), tie), "feat", bit)
            if d == 0 and bit == bits[-1]:
                return held[0], got, beside
            held[d] = held[d] + got.astype(F32)
        held = {d: held[d] for d in stay}


def on_device(
    inputs, norm_gain, w_in, w_out, block_index, segment_ids, teacher_scores, upstream, readout
):
    rows, width = inputs.shape
    nt, nf = lax.axis_size("tok"), lax.axis_size("feat")
    nj, kb = block_index.shape
    hidden = w_in.shape[1]
    fb = width // BLK
    depth = w_in.shape[0]
    tokens = rows * nf
    grad_scale = 1.0 / math.sqrt(tokens * nt)
    bits = bits_of(nt)[1:]
    orders = (bits, bits[::-1])
    feat_bits = bits_of(nf)
    place = lax.axis_index("tok").astype(jnp.int32).reshape(1)
    gain_row, readout_row = norm_gain.reshape(1, width), readout.reshape(1, width)
    flops = 2 * tokens * hidden * kb * BLK
    sds = jax.ShapeDtypeStruct
    scalars = [(SM, block_index), (SM, place)]

    xs = gather_feat(inputs, feat_bits)
    near, far = xs[1], xs[feat_bits[-1]]
    upstream_far = swap(after(upstream, near, far), "feat", feat_bits[-1])
    ups = gather_feat(upstream, feat_bits, upstream_far)
    parts, masks = gather_tok(
        w_in, w_out, bits, ((near, far), [upstream_far], xs[2:])
    )
    parts = [(HBM, p) for p in parts]

    by_feature = pltpu.VMEM((fb, tokens, BLK), BF16)
    by_hidden = pltpu.VMEM((nj, tokens, BLK), BF16)
    weight = pltpu.VMEM((kb * BLK, hidden), BF16)
    summed = pltpu.VMEM((fb, tokens, BLK), F32)
    piece = sds((rows, width), BF16)

    outs = call(
        functools.partial(forward_kernel, masks, nf),
        [
            (HBM, sds((fb, tokens, BLK), BF16)),
            (HBM, sds((nj, tokens, BLK), BF16)),
            (HBM, sds((nj, tokens, BLK), BF16)),
            (VM, sds((1, tokens + rows), F32)),
        ]
        + [(HBM, piece)] * nf,
        scalars
        + [(HBM, x) for x in xs]
        + [(VM, gain_row), (VM, readout_row), (VM, segment_ids.reshape(1, rows))]
        + parts,
        [
            pltpu.VMEM((nf, rows, width), BF16),
            by_feature,
            by_hidden,
            by_hidden,
            weight,
            weight,
            summed,
            pltpu.VMEM((nf, rows, width), BF16),
            pltpu.SemaphoreType.DMA((nf + 5,)),
        ],
        2 * flops,
    )
    normed, act, dact, here = outs[:4]
    branch = outs[4:]

    upper, turn = call(
        functools.partial(upper_kernel, masks, nf),
        [
            (HBM, sds((nj, tokens, BLK), BF16)),
            (VM, sds((1, hidden), F32)),
        ],
        scalars + [(HBM, u) for u in ups] + [(VM, readout_row)] + parts,
        [
            pltpu.VMEM((nf, rows, width), BF16),
            by_feature,
            weight,
            by_hidden,
            pltpu.SemaphoreType.DMA((nf + 2,)),
        ],
        flops,
    )
    for step, bit in enumerate(feat_bits):
        there = swap(after(here, *ups[1:]) if step == 0 else here, "feat", bit)
        if step == 0:
            branch_near = scatter_near([after(b, there) for b in branch])
        if bit == feat_bits[-1]:
            there = after(there, turn)
        turned = jnp.flip(there[:, :tokens].reshape(nf // (2 * bit), 2, bit * rows), axis=1)
        here = jnp.concatenate(
            [here[:, :tokens] + turned.reshape(1, tokens), here[:, tokens:], there[:, tokens:]],
            axis=1,
        )
    left = swap(here, "tok", 1)
    odd = range(1, nt - 1, 2)
    right = lax.ppermute(here, "tok", [(i, i + 1) for i in odd] + [(i + 1, i) for i in odd])

    branch_near = {d: after(got, turn) for d, got in branch_near.items()}
    half_grads = sds((kb * BLK, hidden), BF16)
    own_coeff, pre_grad, keep, send = call(
        functools.partial(grads_kernel, orders, grad_scale, nf),
        [
            (VM, sds((rows, BLK), F32)),
            (VM, sds((nj, tokens, BLK), BF16)),
            (VM, half_grads),
            (VM, half_grads),
        ],
        scalars
        + [(VM, here), (VM, left), (VM, right), (VM, teacher_scores.reshape(-1, 1)), (VM, turn)]
        + [(VM, readout_row)]
        + [(HBM, a) for a in (upper, dact, normed, act)]
        + [(HBM, u) for u in ups],
        [
            by_hidden,
            by_hidden,
            by_feature,
            by_hidden,
            by_feature,
            pltpu.VMEM((nf, rows, width), BF16),
            pltpu.SemaphoreType.DMA((nf + 4,)),
        ],
        2 * flops,
    )
    back = call(
        functools.partial(back_kernel, masks, nf),
        [(VM, piece)] * nf,
        scalars + [(VM, pre_grad)] + parts,
        [weight, summed, pltpu.SemaphoreType.DMA],
        flops,
    )
    branch_own, branch_got, beside = scatter_far(branch, branch_near, feat_bits, here)
    branch_got = after(branch_got, own_coeff)
    layer_out = (inputs.astype(F32) + (branch_own + branch_got.astype(F32))).astype(BF16)
    send = after(send, branch_got, beside)
    own, got, _ = scatter_far(back, scatter_near(back), feat_bits, branch_got)
    sums = Halving([keep, after(swap(send, "tok", 1), back[1])])
    for pair in zip(bits, bits[::-1]):
        sums.add(swap_tok(sums.away(), *pair))
    grads = sums.total()
    grad_out, grad_in = grads[:depth], grads[depth:]
    got = after(got, grad_out, grad_in)
    (input_grad,) = call(
        finish_kernel,
        [(VM, piece)],
        [
            (VM, a)
            for a in (inputs, gain_row, upstream, readout_row, own_coeff, own, got)
        ],
        [],
        rows * width,
    )
    return (layer_out, input_grad, grad_in, grad_out)


def solution(mesh):
    return jax.shard_map(
        on_device,
        mesh=mesh,
        in_specs=(
            P(("tok", "feat"), None),
            P(),
            P("tok", "feat"),
            P("tok", "feat"),
            P("feat", None),
            P(("tok", "feat")),
            P(),
            P(("tok", "feat"), None),
            P(),
        ),
        out_specs=(
            P(("tok", "feat"), None),
            P(("tok", "feat"), None),
            P("tok", "feat"),
            P("tok", "feat"),
        ),
        check_vma=False,
    )
```

```python
import functools
import math

import jax
import jax.numpy as jnp
from jax import lax
from jax.experimental import pallas as pl
from jax.experimental.pallas import tpu as pltpu
from jax.sharding import PartitionSpec as P

BLK = 128
EPS = 1e-06
LOSS_WEIGHT = 8.0
GELU_A = math.sqrt(2.0 / math.pi)
GELU_B = 0.044715
VMEM_BYTES = 32 * 1024 * 1024
BF16 = jnp.bfloat16
F32 = jnp.float32
NN = (((1,), (0,)), ((), ()))
NT = (((1,), (1,)), ((), ()))
TN = (((0,), (0,)), ((), ()))


def dot(a, b, dims=NN):
    return lax.dot_general(a, b, dims, preferred_element_type=F32)


def block(b):
    return slice(b * BLK, (b + 1) * BLK)


def column(j):
    return pl.ds(pl.multiple_of(j * BLK, BLK), BLK)


def bits_of(n):
    return [1 << b for b in range(n.bit_length() - 1)]


def three_terms(row):
    hi = row.astype(BF16)
    rest = row - hi.astype(F32)
    mid = rest.astype(BF16)
    low = (rest - mid.astype(F32)).astype(BF16)
    pad = jnp.zeros((8 - 3, row.shape[1]), F32).astype(BF16)
    return jnp.concatenate([hi, mid, low, pad], axis=0)


def load_weight(place, parts, masks, which, whole, sem):
    core = place[0] & 1
    for part, ms in zip(parts, masks):
        depth = part.shape[0] // (2 * len(ms))
        for i, (even, odd) in enumerate(ms):
            owner = place[0] ^ jnp.where(core == 0, even, odd)
            at = pl.multiple_of(owner * depth, depth)
            pltpu.make_async_copy(
                part.at[pl.ds((2 * i + which) * depth, depth)], whole.at[pl.ds(at, depth)], sem
            ).start()
    return lambda: pltpu.make_async_copy(whole, whole, sem).wait()


def load(src, dst, sem):
    copy = pltpu.make_async_copy(src, dst, sem)
    copy.start()
    return copy.wait


def loop(nj, unroll=8):
    return pl.loop(0, nj, unroll=math.gcd(nj, unroll))


def spread(acc, outs, rows):
    for b in range(acc.shape[0]):
        part = acc[b].astype(BF16)
        for d, out in enumerate(outs):
            out[:, block(b)] = part[d * rows : (d + 1) * rows]


def forward_kernel(masks, nf, *refs):
    idx, place = refs[:2]
    xs, refs = refs[2 : 2 + nf], refs[2 + nf:]
    gain, readout, ids = refs[:3]
    parts, refs = refs[3 : 3 + len(masks)], refs[3 + len(masks):]
    normed_out, act_out, dact_out, score = refs[:4]
    branch_out, refs = refs[4 : 4 + nf], refs[4 + nf:]
    xbuf, normed, act, dact, win, wout, acc, branch, sems = refs
    rows = ids.shape[1]
    fb = normed.shape[0]
    nj, kb = idx.shape
    waits = [load(xs[d], xbuf.at[d], sems.at[d]) for d in range(nf)]
    win_wait = load_weight(place, parts, masks, 0, win, sems.at[nf])
    wout_wait = load_weight(place, parts, masks, 1, wout, sems.at[nf + 1])
    acc[...] = jnp.zeros_like(acc)
    own = jnp.zeros((8, rows), F32)
    for d in range(nf):
        waits[d]()
        x = xbuf[d].astype(F32)
        inv = lax.rsqrt(jnp.mean(x * x, axis=1, keepdims=True) + EPS)
        n = (x * inv * gain[...]).astype(BF16)
        for b in range(fb):
            normed[b, d * rows : (d + 1) * rows, :] = n[:, block(b)]
            if d == 0:
                own = own + dot(three_terms(readout[:, block(b)]), xbuf[0, :, block(b)], NT)
    normed_wait = load(normed, normed_out, sems.at[nf + 2])
    win_wait()
    wout_wait()

    @loop(nj)
    def _(j):
        which = [idx[j, k] for k in range(kb)]
        picked = jnp.concatenate([normed[w] for w in which], axis=1)
        v = dot(picked, win[:, column(j)])
        v2 = v * v
        t = jnp.tanh(GELU_A * v * (1.0 + GELU_B * v2))
        half = 0.5 * (1.0 + t)
        a = (v * half).astype(BF16)
        act[j] = a
        slope = half + 0.5 * v * (1.0 - t * t) * (GELU_A * (1.0 + 3.0 * GELU_B * v2))
        dact[j] = slope.astype(BF16)
        pltpu.make_async_copy(act.at[j], act_out.at[j], sems.at[nf + 3]).start()
        pltpu.make_async_copy(dact.at[j], dact_out.at[j], sems.at[nf + 4]).start()
        terms = dot(a, wout[:, column(j)], NT)
        for k, w in enumerate(which):
            acc[w] += terms[:, block(k)]

    act_wait = pltpu.make_async_copy(act, act_out, sems.at[nf + 3]).wait
    dact_wait = pltpu.make_async_copy(dact, dact_out, sems.at[nf + 4]).wait
    spread(acc, [branch.at[d] for d in range(nf)], rows)
    waits = [load(branch.at[d], branch_out[d], sems.at[d]) for d in range(nf)]
    total = jnp.zeros((8, nf * rows), F32)
    for b in range(fb):
        total = total + dot(three_terms(readout[:, block(b)]), acc[b].astype(BF16), NT)
    own = jnp.sum(own, axis=0, keepdims=True)
    pad = jnp.zeros((1, (nf - 1) * rows), F32)
    row = jnp.sum(total, axis=0, keepdims=True) + jnp.concatenate([own, pad], axis=1)
    score[...] = jnp.concatenate([row, ids[...].astype(F32) + 1.0], axis=1)
    for wait in waits + [normed_wait, act_wait, dact_wait]:
        wait()


def store_grads(idx, place, orders, scale, pairs, keep, send):
    nj, kb = idx.shape
    count = 2 << len(orders[0])
    depth = kb * BLK // count
    per = BLK // depth
    core = place[0] & 1

    def slot(owner, order):
        m = place[0] ^ owner
        pos = 0
        for bit in order:
            pos = 2 * pos + jnp.where((m & bit) != 0, 1, 0)
        return pos * len(pairs) * depth

    def slots(own):
        return [
            jnp.where(own == 0, slot(2 * q, orders[0]), slot(2 * q, orders[1]))
            for q in range(count // 2)
        ]

    keep_at, send_at = slots(core), slots(1 - core)

    @loop(nj, 4)
    def _(j):
        for which, (left, right) in enumerate(pairs):
            for k in range(kb):
                g = (dot(left[idx[j, k]], right[j], TN) * scale).astype(BF16)
                for half in range(per // 2):
                    q = k * (per // 2) + half
                    even = g[2 * half * depth : (2 * half + 1) * depth]
                    odd = g[(2 * half + 1) * depth : (2 * half + 2) * depth]
                    kept = pl.multiple_of(keep_at[q] + which * depth, depth)
                    sent = pl.multiple_of(send_at[q] + which * depth, depth)
                    keep[pl.ds(kept, depth), column(j)] = jnp.where(core == 0, even, odd)
                    send[pl.ds(sent, depth), column(j)] = jnp.where(core == 0, odd, even)


def upper_kernel(masks, nf, *refs):
    idx, place = refs[:2]
    ups, refs = refs[2 : 2 + nf], refs[2 + nf:]
    readout, refs = refs[0], refs[1:]
    parts, refs = refs[: len(masks)], refs[len(masks):]
    upper_out, turn, ubuf, up, wout, upper, sems = refs
    nj, kb = idx.shape
    fb = up.shape[0]
    rows = ubuf.shape[1]
    waits = [load(ups[d], ubuf.at[d], sems.at[d]) for d in range(nf)]
    wout_wait = load_weight(place, parts, masks, 1, wout, sems.at[nf])
    for d in range(nf):
        waits[d]()
        for b in range(fb):
            up[b, d * rows : (d + 1) * rows, :] = ubuf[d, :, block(b)]
    wout_wait()

    @loop(nj)
    def _(j):
        which = [idx[j, k] for k in range(kb)]
        picked = jnp.concatenate([up[w] for w in which], axis=1)
        turned = jnp.concatenate([three_terms(readout[:, column(w)]) for w in which], axis=1)
        rows_of = jnp.concatenate([picked, turned, jnp.zeros_like(turned)], axis=0)
        both = dot(rows_of, wout[:, column(j)])
        upper[j] = both[: nf * rows].astype(BF16)
        pltpu.make_async_copy(upper.at[j], upper_out.at[j], sems.at[nf + 1]).start()
        turn[:, column(j)] = jnp.sum(both[nf * rows : nf * rows + 8], axis=0, keepdims=True)

    pltpu.make_async_copy(upper, upper_out, sems.at[nf + 1]).wait()


def grads_kernel(orders, scale, nf, *refs):
    idx, place, here, left, right, teacher, turn, readout, upper_in, dact_in, normed_in, act_in = refs[:12]
    ups, refs = refs[12 : 12 + nf], refs[12 + nf:]
    own_coeff, pre_grad, keep, send, upper, dact, normed, act, cot, ubuf, sems = refs
    nj, kb = idx.shape
    rows = ubuf.shape[1]
    tokens = nf * rows
    nseg = teacher.shape[0]
    up_waits = [load(ups[d], ubuf.at[d], sems.at[4 + d]) for d in range(nf)]
    upper_wait = load(upper_in, upper, sems.at[0])
    dact_wait = load(dact_in, dact, sems.at[1])
    normed_wait = load(normed_in, normed, sems.at[2])
    act_wait = load(act_in, act, sems.at[3])
    seg = (lax.broadcasted_iota(jnp.int32, (nseg, tokens), 0) + 1).astype(F32)
    sums = jnp.zeros((nseg, 1), F32)
    counts = jnp.zeros((nseg, 1), F32)
    for group in (here, left, right):
        member = group[:, tokens:] == seg
        sums = sums + jnp.sum(jnp.where(member, group[:, :tokens], 0.0), axis=1, keepdims=True)
        counts = counts + jnp.sum(jnp.where(member, 1.0, 0.0), axis=1, keepdims=True)
    misfit = sums / jnp.maximum(counts, 1.0) - teacher[...]
    coeff = 2.0 * LOSS_WEIGHT * jnp.sum(
        jnp.where(here[:, tokens:] == seg, misfit, 0.0), axis=0, keepdims=True
    )
    across = jnp.transpose(jnp.broadcast_to(coeff, (BLK, tokens)))
    own_coeff[...] = across[:rows]
    for d in range(nf):
        up_waits[d]()
        part = across[d * rows : (d + 1) * rows]
        for b in range(cot.shape[0]):
            c = ubuf[d, :, block(b)].astype(F32) + part * readout[:, block(b)]
            cot[b, d * rows : (d + 1) * rows, :] = c.astype(BF16)
    upper_wait()
    dact_wait()

    @loop(nj)
    def _(j):
        whole = upper[j].astype(F32) + across * turn[:, column(j)]
        pre_grad[j] = (whole * dact[j].astype(F32)).astype(BF16)

    normed_wait()
    act_wait()
    store_grads(idx, place, orders, scale, ((cot, act), (normed, pre_grad)), keep, send)


def back_kernel(masks, nf, *refs):
    idx, place, pre_grad = refs[:3]
    parts, refs = refs[3 : 3 + len(masks)], refs[3 + len(masks):]
    outs, (win, acc, sem) = refs[:nf], refs[nf:]
    nj, kb = idx.shape
    win_wait = load_weight(place, parts, masks, 0, win, sem)
    acc[...] = jnp.zeros_like(acc)
    win_wait()

    @loop(nj)
    def _(j):
        terms = dot(pre_grad[j], win[:, column(j)], NT)
        for k in range(kb):
            acc[idx[j, k]] += terms[:, block(k)]

    spread(acc, outs, outs[0].shape[0])


def finish_kernel(x_ref, gain, upstream, readout, own_coeff, own, other, out):
    x = x_ref[...].astype(F32)
    inv = lax.rsqrt(jnp.mean(x * x, axis=1, keepdims=True) + EPS)
    g = (own[...] + other[...].astype(F32)) * gain[...]
    inner = jnp.mean(g * x, axis=1, keepdims=True)
    back = inv * g - x * (inv * inv * inv) * inner
    for b in range(x.shape[1] // BLK):
        cot = upstream[:, block(b)].astype(F32) + own_coeff[...] * readout[:, block(b)]
        out[:, block(b)] = (cot.astype(BF16).astype(F32) + back[:, block(b)]).astype(BF16)


VM = pl.BlockSpec(memory_space=pltpu.VMEM)
SM = pl.BlockSpec(memory_space=pltpu.SMEM)
HBM = pl.BlockSpec(memory_space=pltpu.HBM)


def call(body, outs, args, scratch, flops):
    return pl.pallas_call(
        body,
        out_shape=[pltpu.HBM(o.shape, o.dtype) if m is HBM else o for m, o in outs],
        in_specs=[m for m, _ in args],
        out_specs=[m for m, _ in outs],
        scratch_shapes=scratch,
        compiler_params=pltpu.CompilerParams(vmem_limit_bytes=VMEM_BYTES),
        cost_estimate=pl.CostEstimate(
            flops=flops,
            bytes_accessed=sum(math.prod(o.shape) * o.dtype.itemsize for _, o in outs),
            transcendentals=0,
        ),
    )(*[pltpu.with_memory_space_constraint(a, pltpu.HBM) if m is HBM else a for m, a in args])


def stack_kernel(*refs):
    at = 0
    for p in refs[:-1]:
        refs[-1][at : at + p.shape[0]] = p[...]
        at += p.shape[0]


def stack(parts):
    rows = sum(p.shape[0] for p in parts)
    whole = jax.ShapeDtypeStruct((rows,) + parts[0].shape[1:], parts[0].dtype)
    return call(
        stack_kernel, [(VM, whole)], [(VM, p) for p in parts], [], 0
    )[0]


def swap(value, axis, mask):
    n = lax.axis_size(axis)
    return lax.ppermute(value, axis, [(i, i ^ mask) for i in range(n)])


def swap_tok(value, even, odd):
    n = lax.axis_size("tok")
    return lax.ppermute(value, "tok", [(i, i ^ (odd if i & 1 else even)) for i in range(n)])


def after(value, *others):
    return lax.optimization_barrier((value, *others))[0]


def gather_tok(w_in, w_out, bits, ties):
    held, masks = [w_in, w_out], [[(0, 0)]]
    for step, (even, odd) in enumerate(zip(bits, bits[::-1])):
        if step == 0 and len(bits) > 1:
            own = stack(held)
            held = [own] + [swap_tok(after(h, own), even, odd) for h in held]
            masks = [[(0, 0), (even, odd)]]
            continue
        if step == len(bits) - 1:
            held = [after(held[0], *ties[0])] + held[1:]
        whole = stack(held)
        flat = [m for ms in masks for m in ms]
        held = [whole, swap_tok(whole, even, odd)]
        masks = [flat, [(a ^ even, b ^ odd) for a, b in flat]]
    other = [swap(after(h, *tie), "tok", 1) for h, tie in zip(held, ties[1:])]
    return held + other, masks + [[(b ^ 1, a ^ 1) for a, b in ms] for ms in masks]


class Halving:
    def __init__(self, terms):
        self.terms = terms

    def total(self):
        return functools.reduce(lambda a, b: a + b, [t.astype(F32) for t in self.terms])

    def away(self):
        half = self.terms[0].shape[0] // 2
        sent = Halving([t[half:] for t in self.terms]).total().astype(BF16)
        self.terms = [t[:half] for t in self.terms]
        return sent

    def add(self, term):
        self.terms.append(term)


def gather_feat(own, bits, far=None):
    held = {0: own}
    for bit in bits[::-1]:
        if bit == bits[-1] and far is not None:
            held[bit] = far
        else:
            held.update({
                m ^ bit: swap(held[m] if far is None else after(held[m], far), "feat", bit)
                for m in sorted(held)
            })
    return [held[d] for d in range(2 * bits[-1])]


def scatter_near(parts):
    return {d: swap(parts[d + 1], "feat", 1) for d in range(len(parts) - 2, 0, -2)}


def scatter_far(parts, held, bits, tie):
    firsts = [held[d] for d in sorted(held)]
    held = {d: parts[d].astype(F32) + got.astype(F32) for d, got in held.items()}
    beside = swap(after(parts[1], *firsts), "feat", 1)
    held[0] = parts[0].astype(F32) + beside.astype(F32)
    for bit in bits[1:]:
        stay = [d for d in held if not d & bit]
        for d in sorted(stay, reverse=True):
            got = swap(after(held[d | bit].astype(BF16), tie), "feat", bit)
            if d == 0 and bit == bits[-1]:
                return held[0], got, beside
            held[d] = held[d] + got.astype(F32)
        held = {d: held[d] for d in stay}


def on_device(
    inputs, norm_gain, w_in, w_out, block_index, segment_ids, teacher_scores, upstream, readout
):
    rows, width = inputs.shape
    nt, nf = lax.axis_size("tok"), lax.axis_size("feat")
    nj, kb = block_index.shape
    hidden = w_in.shape[1]
    fb = width // BLK
    depth = w_in.shape[0]
    tokens = rows * nf
    grad_scale = 1.0 / math.sqrt(tokens * nt)
    bits = bits_of(nt)[1:]
    orders = (bits, bits[::-1])
    feat_bits = bits_of(nf)
    place = lax.axis_index("tok").astype(jnp.int32).reshape(1)
    gain_row, readout_row = norm_gain.reshape(1, width), readout.reshape(1, width)
    flops = 2 * tokens * hidden * kb * BLK
    sds = jax.ShapeDtypeStruct
    scalars = [(SM, block_index), (SM, place)]

    xs = gather_feat(inputs, feat_bits)
    near, far = xs[1], xs[feat_bits[-1]]
    upstream_far = swap(after(upstream, near, far), "feat", feat_bits[-1])
    ups = gather_feat(upstream, feat_bits, upstream_far)
    parts, masks = gather_tok(
        w_in, w_out, bits, ((near, far), [upstream_far], xs[2:])
    )
    parts = [(HBM, p) for p in parts]

    by_feature = pltpu.VMEM((fb, tokens, BLK), BF16)
    by_hidden = pltpu.VMEM((nj, tokens, BLK), BF16)
    weight = pltpu.VMEM((kb * BLK, hidden), BF16)
    summed = pltpu.VMEM((fb, tokens, BLK), F32)
    piece = sds((rows, width), BF16)

    outs = call(
        functools.partial(forward_kernel, masks, nf),
        [
            (HBM, sds((fb, tokens, BLK), BF16)),
            (HBM, sds((nj, tokens, BLK), BF16)),
            (HBM, sds((nj, tokens, BLK), BF16)),
            (VM, sds((1, tokens + rows), F32)),
        ]
        + [(HBM, piece)] * nf,
        scalars
        + [(HBM, x) for x in xs]
        + [(VM, gain_row), (VM, readout_row), (VM, segment_ids.reshape(1, rows))]
        + parts,
        [
            pltpu.VMEM((nf, rows, width), BF16),
            by_feature,
            by_hidden,
            by_hidden,
            weight,
            weight,
            summed,
            pltpu.VMEM((nf, rows, width), BF16),
            pltpu.SemaphoreType.DMA((nf + 5,)),
        ],
        2 * flops,
    )
    normed, act, dact, here = outs[:4]
    branch = outs[4:]

    upper, turn = call(
        functools.partial(upper_kernel, masks, nf),
        [
            (HBM, sds((nj, tokens, BLK), BF16)),
            (VM, sds((1, hidden), F32)),
        ],
        scalars + [(HBM, u) for u in ups] + [(VM, readout_row)] + parts,
        [
            pltpu.VMEM((nf, rows, width), BF16),
            by_feature,
            weight,
            by_hidden,
            pltpu.SemaphoreType.DMA((nf + 2,)),
        ],
        flops,
    )
    for step, bit in enumerate(feat_bits):
        there = swap(after(here, *ups[1:]) if step == 0 else here, "feat", bit)
        if step == 0:
            branch_near = scatter_near([after(b, there) for b in branch])
        if bit == feat_bits[-1]:
            there = after(there, turn)
        turned = jnp.flip(there[:, :tokens].reshape(nf // (2 * bit), 2, bit * rows), axis=1)
        here = jnp.concatenate(
            [here[:, :tokens] + turned.reshape(1, tokens), here[:, tokens:], there[:, tokens:]],
            axis=1,
        )
    left = swap(here, "tok", 1)
    odd = range(1, nt - 1, 2)
    right = lax.ppermute(here, "tok", [(i, i + 1) for i in odd] + [(i + 1, i) for i in odd])

    branch_near = {d: after(got, turn) for d, got in branch_near.items()}
    half_grads = sds((kb * BLK, hidden), BF16)
    own_coeff, pre_grad, keep, send = call(
        functools.partial(grads_kernel, orders, grad_scale, nf),
        [
            (VM, sds((rows, BLK), F32)),
            (VM, sds((nj, tokens, BLK), BF16)),
            (VM, half_grads),
            (VM, half_grads),
        ],
        scalars
        + [(VM, here), (VM, left), (VM, right), (VM, teacher_scores.reshape(-1, 1)), (VM, turn)]
        + [(VM, readout_row)]
        + [(HBM, a) for a in (upper, dact, normed, act)]
        + [(HBM, u) for u in ups],
        [
            by_hidden,
            by_hidden,
            by_feature,
            by_hidden,
            by_feature,
            pltpu.VMEM((nf, rows, width), BF16),
            pltpu.SemaphoreType.DMA((nf + 4,)),
        ],
        2 * flops,
    )
    back = call(
        functools.partial(back_kernel, masks, nf),
        [(VM, piece)] * nf,
        scalars + [(VM, pre_grad)] + parts,
        [weight, summed, pltpu.SemaphoreType.DMA],
        flops,
    )
    branch_own, branch_got, beside = scatter_far(branch, branch_near, feat_bits, here)
    branch_got = after(branch_got, own_coeff)
    layer_out = (inputs.astype(F32) + (branch_own + branch_got.astype(F32))).astype(BF16)
    send = after(send, branch_got, beside)
    own, got, _ = scatter_far(back, scatter_near(back), feat_bits, branch_got)
    sums = Halving([keep, after(swap(send, "tok", 1), back[1])])
    for pair in zip(bits, bits[::-1]):
        sums.add(swap_tok(sums.away(), *pair))
    grads = sums.total()
    grad_out, grad_in = grads[:depth], grads[depth:]
    got = after(got, grad_out, grad_in)
    (input_grad,) = call(
        finish_kernel,
        [(VM, piece)],
        [
            (VM, a)
            for a in (inputs, gain_row, upstream, readout_row, own_coeff, own, got)
        ],
        [],
        rows * width,
    )
    return (layer_out, input_grad, grad_in, grad_out)


def solution(mesh):
    return jax.shard_map(
        on_device,
        mesh=mesh,
        in_specs=(
            P(("tok", "feat"), None),
            P(),
            P("tok", "feat"),
            P("tok", "feat"),
            P("feat", None),
            P(("tok", "feat")),
            P(),
            P(("tok", "feat"), None),
            P(),
        ),
        out_specs=(
            P(("tok", "feat"), None),
            P(("tok", "feat"), None),
            P("tok", "feat"),
            P("tok", "feat"),
        ),
        check_vma=False,
    )
```

```python
import functools
import math

import jax
import jax.numpy as jnp
from jax import lax
from jax.experimental import pallas as pl
from jax.experimental.pallas import tpu as pltpu
from jax.sharding import PartitionSpec as P

BLK = 128
EPS = 1e-06
LOSS_WEIGHT = 8.0
GELU_A = math.sqrt(2.0 / math.pi)
GELU_B = 0.044715
VMEM_BYTES = 32 * 1024 * 1024
BF16 = jnp.bfloat16
F32 = jnp.float32
NN = (((1,), (0,)), ((), ()))
NT = (((1,), (1,)), ((), ()))
TN = (((0,), (0,)), ((), ()))


def dot(a, b, dims=NN):
    return lax.dot_general(a, b, dims, preferred_element_type=F32)


def block(b):
    return slice(b * BLK, (b + 1) * BLK)


def column(j):
    return pl.ds(pl.multiple_of(j * BLK, BLK), BLK)


def bits_of(n):
    return [1 << b for b in range(n.bit_length() - 1)]


def three_terms(row):
    hi = row.astype(BF16)
    rest = row - hi.astype(F32)
    mid = rest.astype(BF16)
    low = (rest - mid.astype(F32)).astype(BF16)
    pad = jnp.zeros((8 - 3, row.shape[1]), F32).astype(BF16)
    return jnp.concatenate([hi, mid, low, pad], axis=0)


def load_weight(place, parts, masks, which, whole, sem):
    core = place[0] & 1
    for part, ms in zip(parts, masks):
        depth = part.shape[0] // (2 * len(ms))
        for i, (even, odd) in enumerate(ms):
            owner = place[0] ^ jnp.where(core == 0, even, odd)
            at = pl.multiple_of(owner * depth, depth)
            pltpu.make_async_copy(
                part.at[pl.ds((2 * i + which) * depth, depth)], whole.at[pl.ds(at, depth)], sem
            ).start()
    return lambda: pltpu.make_async_copy(whole, whole, sem).wait()


def load(src, dst, sem):
    copy = pltpu.make_async_copy(src, dst, sem)
    copy.start()
    return copy.wait


def loop(nj, unroll=8):
    return pl.loop(0, nj, unroll=math.gcd(nj, unroll))


def spread(acc, outs, rows):
    for b in range(acc.shape[0]):
        part = acc[b].astype(BF16)
        for d, out in enumerate(outs):
            out[:, block(b)] = part[d * rows : (d + 1) * rows]


def forward_kernel(masks, nf, *refs):
    idx, place = refs[:2]
    xs, refs = refs[2 : 2 + nf], refs[2 + nf:]
    gain, readout, ids = refs[:3]
    parts, refs = refs[3 : 3 + len(masks)], refs[3 + len(masks):]
    normed_out, act_out, dact_out, score = refs[:4]
    branch_out, refs = refs[4 : 4 + nf], refs[4 + nf:]
    xbuf, normed, act, dact, win, wout, acc, branch, sems = refs
    rows = ids.shape[1]
    fb = normed.shape[0]
    nj, kb = idx.shape
    waits = [load(xs[d], xbuf.at[d], sems.at[d]) for d in range(nf)]
    win_wait = load_weight(place, parts, masks, 0, win, sems.at[nf])
    wout_wait = load_weight(place, parts, masks, 1, wout, sems.at[nf + 1])
    acc[...] = jnp.zeros_like(acc)
    own = jnp.zeros((8, rows), F32)
    for d in range(nf):
        waits[d]()
        x = xbuf[d].astype(F32)
        inv = lax.rsqrt(jnp.mean(x * x, axis=1, keepdims=True) + EPS)
        n = (x * inv * gain[...]).astype(BF16)
        for b in range(fb):
            normed[b, d * rows : (d + 1) * rows, :] = n[:, block(b)]
            if d == 0:
                own = own + dot(three_terms(readout[:, block(b)]), xbuf[0, :, block(b)], NT)
    normed_wait = load(normed, normed_out, sems.at[nf + 2])
    win_wait()
    wout_wait()

    @loop(nj)
    def _(j):
        which = [idx[j, k] for k in range(kb)]
        picked = jnp.concatenate([normed[w] for w in which], axis=1)
        v = dot(picked, win[:, column(j)])
        v2 = v * v
        t = jnp.tanh(GELU_A * v * (1.0 + GELU_B * v2))
        half = 0.5 * (1.0 + t)
        a = (v * half).astype(BF16)
        act[j] = a
        slope = half + 0.5 * v * (1.0 - t * t) * (GELU_A * (1.0 + 3.0 * GELU_B * v2))
        dact[j] = slope.astype(BF16)
        pltpu.make_async_copy(act.at[j], act_out.at[j], sems.at[nf + 3]).start()
        pltpu.make_async_copy(dact.at[j], dact_out.at[j], sems.at[nf + 4]).start()
        terms = dot(a, wout[:, column(j)], NT)
        for k, w in enumerate(which):
            acc[w] += terms[:, block(k)]

    act_wait = pltpu.make_async_copy(act, act_out, sems.at[nf + 3]).wait
    dact_wait = pltpu.make_async_copy(dact, dact_out, sems.at[nf + 4]).wait
    spread(acc, [branch.at[d] for d in range(nf)], rows)
    waits = [load(branch.at[d], branch_out[d], sems.at[d]) for d in range(nf)]
    total = jnp.zeros((8, nf * rows), F32)
    for b in range(fb):
        total = total + dot(three_terms(readout[:, block(b)]), acc[b].astype(BF16), NT)
    own = jnp.sum(own, axis=0, keepdims=True)
    pad = jnp.zeros((1, (nf - 1) * rows), F32)
    row = jnp.sum(total, axis=0, keepdims=True) + jnp.concatenate([own, pad], axis=1)
    score[...] = jnp.concatenate([row, ids[...].astype(F32) + 1.0], axis=1)
    for wait in waits + [normed_wait, act_wait, dact_wait]:
        wait()


def store_grads(idx, place, orders, scale, pairs, keep, send):
    nj, kb = idx.shape
    count = 2 << len(orders[0])
    depth = kb * BLK // count
    per = BLK // depth
    core = place[0] & 1

    def slot(owner, order):
        m = place[0] ^ owner
        pos = 0
        for bit in order:
            pos = 2 * pos + jnp.where((m & bit) != 0, 1, 0)
        return pos * len(pairs) * depth

    def slots(own):
        return [
            jnp.where(own == 0, slot(2 * q, orders[0]), slot(2 * q, orders[1]))
            for q in range(count // 2)
        ]

    keep_at, send_at = slots(core), slots(1 - core)

    @loop(nj, 4)
    def _(j):
        for which, (left, right) in enumerate(pairs):
            for k in range(kb):
                g = (dot(left[idx[j, k]], right[j], TN) * scale).astype(BF16)
                for half in range(per // 2):
                    q = k * (per // 2) + half
                    even = g[2 * half * depth : (2 * half + 1) * depth]
                    odd = g[(2 * half + 1) * depth : (2 * half + 2) * depth]
                    kept = pl.multiple_of(keep_at[q] + which * depth, depth)
                    sent = pl.multiple_of(send_at[q] + which * depth, depth)
                    keep[pl.ds(kept, depth), column(j)] = jnp.where(core == 0, even, odd)
                    send[pl.ds(sent, depth), column(j)] = jnp.where(core == 0, odd, even)


def upper_kernel(masks, nf, *refs):
    idx, place = refs[:2]
    ups, refs = refs[2 : 2 + nf], refs[2 + nf:]
    readout, refs = refs[0], refs[1:]
    parts, refs = refs[: len(masks)], refs[len(masks):]
    upper_out, turn, ubuf, up, wout, upper, sems = refs
    nj, kb = idx.shape
    fb = up.shape[0]
    rows = ubuf.shape[1]
    waits = [load(ups[d], ubuf.at[d], sems.at[d]) for d in range(nf)]
    wout_wait = load_weight(place, parts, masks, 1, wout, sems.at[nf])
    for d in range(nf):
        waits[d]()
        for b in range(fb):
            up[b, d * rows : (d + 1) * rows, :] = ubuf[d, :, block(b)]
    wout_wait()

    @loop(nj)
    def _(j):
        which = [idx[j, k] for k in range(kb)]
        picked = jnp.concatenate([up[w] for w in which], axis=1)
        turned = jnp.concatenate([three_terms(readout[:, column(w)]) for w in which], axis=1)
        rows_of = jnp.concatenate([picked, turned, jnp.zeros_like(turned)], axis=0)
        both = dot(rows_of, wout[:, column(j)])
        upper[j] = both[: nf * rows].astype(BF16)
        pltpu.make_async_copy(upper.at[j], upper_out.at[j], sems.at[nf + 1]).start()
        turn[:, column(j)] = jnp.sum(both[nf * rows : nf * rows + 8], axis=0, keepdims=True)

    pltpu.make_async_copy(upper, upper_out, sems.at[nf + 1]).wait()


def grads_kernel(masks, orders, scale, nf, *refs):
    idx, place, here, left, right, teacher, turn, readout, upper_in, dact_in, normed_in, act_in = refs[:12]
    ups, refs = refs[12 : 12 + nf], refs[12 + nf:]
    parts, refs = refs[: len(masks)], refs[len(masks):]
    own_coeff, pre_grad, keep, send, win, upper, dact, normed, act, cot, ubuf, sems = refs
    nj, kb = idx.shape
    rows = ubuf.shape[1]
    tokens = nf * rows
    nseg = teacher.shape[0]
    up_waits = [load(ups[d], ubuf.at[d], sems.at[4 + d]) for d in range(nf)]
    upper_wait = load(upper_in, upper, sems.at[0])
    dact_wait = load(dact_in, dact, sems.at[1])
    normed_wait = load(normed_in, normed, sems.at[2])
    act_wait = load(act_in, act, sems.at[3])
    win_wait = load_weight(place, parts, masks, 0, win, sems.at[4 + nf])
    seg = (lax.broadcasted_iota(jnp.int32, (nseg, tokens), 0) + 1).astype(F32)
    sums = jnp.zeros((nseg, 1), F32)
    counts = jnp.zeros((nseg, 1), F32)
    for group in (here, left, right):
        member = group[:, tokens:] == seg
        sums = sums + jnp.sum(jnp.where(member, group[:, :tokens], 0.0), axis=1, keepdims=True)
        counts = counts + jnp.sum(jnp.where(member, 1.0, 0.0), axis=1, keepdims=True)
    misfit = sums / jnp.maximum(counts, 1.0) - teacher[...]
    coeff = 2.0 * LOSS_WEIGHT * jnp.sum(
        jnp.where(here[:, tokens:] == seg, misfit, 0.0), axis=0, keepdims=True
    )
    across = jnp.transpose(jnp.broadcast_to(coeff, (BLK, tokens)))
    own_coeff[...] = across[:rows]
    for d in range(nf):
        up_waits[d]()
        part = across[d * rows : (d + 1) * rows]
        for b in range(cot.shape[0]):
            c = ubuf[d, :, block(b)].astype(F32) + part * readout[:, block(b)]
            cot[b, d * rows : (d + 1) * rows, :] = c.astype(BF16)
    upper_wait()
    dact_wait()

    @loop(nj)
    def _(j):
        whole = upper[j].astype(F32) + across * turn[:, column(j)]
        pre_grad[j] = (whole * dact[j].astype(F32)).astype(BF16)

    normed_wait()
    act_wait()
    store_grads(idx, place, orders, scale, ((cot, act), (normed, pre_grad)), keep, send)
    win_wait()


def back_kernel(nf, idx, pre_grad, win, *refs):
    outs, acc = refs[:nf], refs[nf]
    nj, kb = idx.shape
    acc[...] = jnp.zeros_like(acc)

    @loop(nj)
    def _(j):
        terms = dot(pre_grad[j], win[:, column(j)], NT)
        for k in range(kb):
            acc[idx[j, k]] += terms[:, block(k)]

    spread(acc, outs, outs[0].shape[0])


def finish_kernel(x_ref, gain, upstream, readout, own_coeff, own, other, out):
    x = x_ref[...].astype(F32)
    inv = lax.rsqrt(jnp.mean(x * x, axis=1, keepdims=True) + EPS)
    g = (own[...] + other[...].astype(F32)) * gain[...]
    inner = jnp.mean(g * x, axis=1, keepdims=True)
    back = inv * g - x * (inv * inv * inv) * inner
    for b in range(x.shape[1] // BLK):
        cot = upstream[:, block(b)].astype(F32) + own_coeff[...] * readout[:, block(b)]
        out[:, block(b)] = (cot.astype(BF16).astype(F32) + back[:, block(b)]).astype(BF16)


VM = pl.BlockSpec(memory_space=pltpu.VMEM)
SM = pl.BlockSpec(memory_space=pltpu.SMEM)
HBM = pl.BlockSpec(memory_space=pltpu.HBM)


def call(body, outs, args, scratch, flops):
    return pl.pallas_call(
        body,
        out_shape=[pltpu.HBM(o.shape, o.dtype) if m is HBM else o for m, o in outs],
        in_specs=[m for m, _ in args],
        out_specs=[m for m, _ in outs],
        scratch_shapes=scratch,
        compiler_params=pltpu.CompilerParams(vmem_limit_bytes=VMEM_BYTES),
        cost_estimate=pl.CostEstimate(
            flops=flops,
            bytes_accessed=sum(math.prod(o.shape) * o.dtype.itemsize for _, o in outs),
            transcendentals=0,
        ),
    )(*[pltpu.with_memory_space_constraint(a, pltpu.HBM) if m is HBM else a for m, a in args])


def stack_kernel(*refs):
    at = 0
    for p in refs[:-1]:
        refs[-1][at : at + p.shape[0]] = p[...]
        at += p.shape[0]


def stack(parts):
    rows = sum(p.shape[0] for p in parts)
    whole = jax.ShapeDtypeStruct((rows,) + parts[0].shape[1:], parts[0].dtype)
    return call(
        stack_kernel, [(VM, whole)], [(VM, p) for p in parts], [], 0
    )[0]


def swap(value, axis, mask):
    n = lax.axis_size(axis)
    return lax.ppermute(value, axis, [(i, i ^ mask) for i in range(n)])


def swap_tok(value, even, odd):
    n = lax.axis_size("tok")
    return lax.ppermute(value, "tok", [(i, i ^ (odd if i & 1 else even)) for i in range(n)])


def after(value, *others):
    return lax.optimization_barrier((value, *others))[0]


def gather_tok(w_in, w_out, bits, ties):
    held, masks = [w_in, w_out], [[(0, 0)]]
    for step, (even, odd) in enumerate(zip(bits, bits[::-1])):
        if step == 0 and len(bits) > 1:
            own = stack(held)
            held = [own] + [swap_tok(after(h, own), even, odd) for h in held]
            masks = [[(0, 0), (even, odd)]]
            continue
        if step == len(bits) - 1:
            held = [after(held[0], *ties[0])] + held[1:]
        whole = stack(held)
        flat = [m for ms in masks for m in ms]
        held = [whole, swap_tok(whole, even, odd)]
        masks = [flat, [(a ^ even, b ^ odd) for a, b in flat]]
    other = [swap(after(h, *tie), "tok", 1) for h, tie in zip(held, ties[1:])]
    return held + other, masks + [[(b ^ 1, a ^ 1) for a, b in ms] for ms in masks]


class Halving:
    def __init__(self, terms):
        self.terms = terms

    def total(self):
        return functools.reduce(lambda a, b: a + b, [t.astype(F32) for t in self.terms])

    def away(self):
        half = self.terms[0].shape[0] // 2
        sent = Halving([t[half:] for t in self.terms]).total().astype(BF16)
        self.terms = [t[:half] for t in self.terms]
        return sent

    def add(self, term):
        self.terms.append(term)


def gather_feat(own, bits, far=None):
    held = {0: own}
    for bit in bits[::-1]:
        if bit == bits[-1] and far is not None:
            held[bit] = far
        else:
            held.update({
                m ^ bit: swap(held[m] if far is None else after(held[m], far), "feat", bit)
                for m in sorted(held)
            })
    return [held[d] for d in range(2 * bits[-1])]


def scatter_near(parts):
    return {d: swap(parts[d + 1], "feat", 1) for d in range(len(parts) - 2, 0, -2)}


def scatter_far(parts, held, bits, tie):
    firsts = [held[d] for d in sorted(held)]
    held = {d: parts[d].astype(F32) + got.astype(F32) for d, got in held.items()}
    beside = swap(after(parts[1], *firsts), "feat", 1)
    held[0] = parts[0].astype(F32) + beside.astype(F32)
    for bit in bits[1:]:
        stay = [d for d in held if not d & bit]
        for d in sorted(stay, reverse=True):
            got = swap(after(held[d | bit].astype(BF16), tie), "feat", bit)
            if d == 0 and bit == bits[-1]:
                return held[0], got, beside
            held[d] = held[d] + got.astype(F32)
        held = {d: held[d] for d in stay}


def on_device(
    inputs, norm_gain, w_in, w_out, block_index, segment_ids, teacher_scores, upstream, readout
):
    rows, width = inputs.shape
    nt, nf = lax.axis_size("tok"), lax.axis_size("feat")
    nj, kb = block_index.shape
    hidden = w_in.shape[1]
    fb = width // BLK
    depth = w_in.shape[0]
    tokens = rows * nf
    grad_scale = 1.0 / math.sqrt(tokens * nt)
    bits = bits_of(nt)[1:]
    orders = (bits, bits[::-1])
    feat_bits = bits_of(nf)
    place = lax.axis_index("tok").astype(jnp.int32).reshape(1)
    gain_row, readout_row = norm_gain.reshape(1, width), readout.reshape(1, width)
    flops = 2 * tokens * hidden * kb * BLK
    sds = jax.ShapeDtypeStruct
    scalars = [(SM, block_index), (SM, place)]

    xs = gather_feat(inputs, feat_bits)
    near, far = xs[1], xs[feat_bits[-1]]
    upstream_far = swap(after(upstream, near, far), "feat", feat_bits[-1])
    ups = gather_feat(upstream, feat_bits, upstream_far)
    parts, masks = gather_tok(
        w_in, w_out, bits, ((near, far), [upstream_far], xs[2:])
    )
    parts = [(HBM, p) for p in parts]

    by_feature = pltpu.VMEM((fb, tokens, BLK), BF16)
    by_hidden = pltpu.VMEM((nj, tokens, BLK), BF16)
    weight = pltpu.VMEM((kb * BLK, hidden), BF16)
    summed = pltpu.VMEM((fb, tokens, BLK), F32)
    piece = sds((rows, width), BF16)

    outs = call(
        functools.partial(forward_kernel, masks, nf),
        [
            (HBM, sds((fb, tokens, BLK), BF16)),
            (HBM, sds((nj, tokens, BLK), BF16)),
            (HBM, sds((nj, tokens, BLK), BF16)),
            (VM, sds((1, tokens + rows), F32)),
        ]
        + [(HBM, piece)] * nf,
        scalars
        + [(HBM, x) for x in xs]
        + [(VM, gain_row), (VM, readout_row), (VM, segment_ids.reshape(1, rows))]
        + parts,
        [
            pltpu.VMEM((nf, rows, width), BF16),
            by_feature,
            by_hidden,
            by_hidden,
            weight,
            weight,
            summed,
            pltpu.VMEM((nf, rows, width), BF16),
            pltpu.SemaphoreType.DMA((nf + 5,)),
        ],
        2 * flops,
    )
    normed, act, dact, here = outs[:4]
    branch = outs[4:]

    upper, turn = call(
        functools.partial(upper_kernel, masks, nf),
        [
            (HBM, sds((nj, tokens, BLK), BF16)),
            (VM, sds((1, hidden), F32)),
        ],
        scalars + [(HBM, u) for u in ups] + [(VM, readout_row)] + parts,
        [
            pltpu.VMEM((nf, rows, width), BF16),
            by_feature,
            weight,
            by_hidden,
            pltpu.SemaphoreType.DMA((nf + 2,)),
        ],
        flops,
    )
    for step, bit in enumerate(feat_bits):
        there = swap(after(here, *ups[1:]) if step == 0 else here, "feat", bit)
        if step == 0:
            branch_near = scatter_near([after(b, there) for b in branch])
        if bit == feat_bits[-1]:
            there = after(there, turn)
        turned = jnp.flip(there[:, :tokens].reshape(nf // (2 * bit), 2, bit * rows), axis=1)
        here = jnp.concatenate(
            [here[:, :tokens] + turned.reshape(1, tokens), here[:, tokens:], there[:, tokens:]],
            axis=1,
        )
    left = swap(here, "tok", 1)
    odd = range(1, nt - 1, 2)
    right = lax.ppermute(here, "tok", [(i, i + 1) for i in odd] + [(i + 1, i) for i in odd])

    branch_near = {d: after(got, turn) for d, got in branch_near.items()}
    half_grads = sds((kb * BLK, hidden), BF16)
    own_coeff, pre_grad, keep, send, win = call(
        functools.partial(grads_kernel, masks, orders, grad_scale, nf),
        [
            (VM, sds((rows, BLK), F32)),
            (VM, sds((nj, tokens, BLK), BF16)),
            (VM, half_grads),
            (VM, half_grads),
            (VM, sds((kb * BLK, hidden), BF16)),
        ],
        scalars
        + [(VM, here), (VM, left), (VM, right), (VM, teacher_scores.reshape(-1, 1)), (VM, turn)]
        + [(VM, readout_row)]
        + [(HBM, a) for a in (upper, dact, normed, act)]
        + [(HBM, u) for u in ups]
        + parts,
        [
            by_hidden,
            by_hidden,
            by_feature,
            by_hidden,
            by_feature,
            pltpu.VMEM((nf, rows, width), BF16),
            pltpu.SemaphoreType.DMA((nf + 5,)),
        ],
        2 * flops,
    )
    back = call(
        functools.partial(back_kernel, nf),
        [(VM, piece)] * nf,
        [(SM, block_index), (VM, pre_grad), (VM, win)],
        [summed],
        flops,
    )
    branch_own, branch_got, beside = scatter_far(branch, branch_near, feat_bits, here)
    branch_got = after(branch_got, own_coeff)
    layer_out = (inputs.astype(F32) + (branch_own + branch_got.astype(F32))).astype(BF16)
    send = after(send, branch_got, beside)
    own, got, _ = scatter_far(back, scatter_near(back), feat_bits, branch_got)
    sums = Halving([keep, after(swap(send, "tok", 1), back[1])])
    for pair in zip(bits, bits[::-1]):
        sums.add(swap_tok(sums.away(), *pair))
    grads = sums.total()
    grad_out, grad_in = grads[:depth], grads[depth:]
    got = after(got, grad_out, grad_in)
    (input_grad,) = call(
        finish_kernel,
        [(VM, piece)],
        [
            (VM, a)
            for a in (inputs, gain_row, upstream, readout_row, own_coeff, own, got)
        ],
        [],
        rows * width,
    )
    return (layer_out, input_grad, grad_in, grad_out)


def solution(mesh):
    return jax.shard_map(
        on_device,
        mesh=mesh,
        in_specs=(
            P(("tok", "feat"), None),
            P(),
            P("tok", "feat"),
            P("tok", "feat"),
            P("feat", None),
            P(("tok", "feat")),
            P(),
            P(("tok", "feat"), None),
            P(),
        ),
        out_specs=(
            P(("tok", "feat"), None),
            P(("tok", "feat"), None),
            P("tok", "feat"),
            P("tok", "feat"),
        ),
        check_vma=False,
    )
```

```python
import functools
import math

import jax
import jax.numpy as jnp
from jax import lax
from jax.experimental import pallas as pl
from jax.experimental.pallas import tpu as pltpu
from jax.sharding import PartitionSpec as P

BLK = 128
EPS = 1e-06
LOSS_WEIGHT = 8.0
GELU_A = math.sqrt(2.0 / math.pi)
GELU_B = 0.044715
VMEM_BYTES = 32 * 1024 * 1024
BF16 = jnp.bfloat16
F32 = jnp.float32
NN = (((1,), (0,)), ((), ()))
NT = (((1,), (1,)), ((), ()))
TN = (((0,), (0,)), ((), ()))


def dot(a, b, dims=NN):
    return lax.dot_general(a, b, dims, preferred_element_type=F32)


def block(b):
    return slice(b * BLK, (b + 1) * BLK)


def column(j):
    return pl.ds(pl.multiple_of(j * BLK, BLK), BLK)


def bits_of(n):
    return [1 << b for b in range(n.bit_length() - 1)]


def three_terms(row):
    hi = row.astype(BF16)
    rest = row - hi.astype(F32)
    mid = rest.astype(BF16)
    low = (rest - mid.astype(F32)).astype(BF16)
    pad = jnp.zeros((8 - 3, row.shape[1]), F32).astype(BF16)
    return jnp.concatenate([hi, mid, low, pad], axis=0)


def load_weight(place, parts, masks, which, whole, sem):
    core = place[0] & 1
    for part, ms in zip(parts, masks):
        depth = part.shape[0] // (2 * len(ms))
        for i, (even, odd) in enumerate(ms):
            owner = place[0] ^ jnp.where(core == 0, even, odd)
            at = pl.multiple_of(owner * depth, depth)
            pltpu.make_async_copy(
                part.at[pl.ds((2 * i + which) * depth, depth)], whole.at[pl.ds(at, depth)], sem
            ).start()
    return lambda: pltpu.make_async_copy(whole, whole, sem).wait()


def load(src, dst, sem):
    copy = pltpu.make_async_copy(src, dst, sem)
    copy.start()
    return copy.wait


def loop(nj, unroll=8):
    return pl.loop(0, nj, unroll=math.gcd(nj, unroll))


def spread(acc, outs, rows):
    for b in range(acc.shape[0]):
        part = acc[b].astype(BF16)
        for d, out in enumerate(outs):
            out[:, block(b)] = part[d * rows : (d + 1) * rows]


def forward_kernel(masks, nf, *refs):
    idx, place = refs[:2]
    xs, refs = refs[2 : 2 + nf], refs[2 + nf:]
    gain, readout, ids = refs[:3]
    parts, refs = refs[3 : 3 + len(masks)], refs[3 + len(masks):]
    normed_out, act_out, dact_out, score = refs[:4]
    branch_out, refs = refs[4 : 4 + nf], refs[4 + nf:]
    xbuf, normed, act, dact, win, wout, acc, branch, sems = refs
    rows = ids.shape[1]
    fb = normed.shape[0]
    nj, kb = idx.shape
    waits = [load(xs[d], xbuf.at[d], sems.at[d]) for d in range(nf)]
    win_wait = load_weight(place, parts, masks, 0, win, sems.at[nf])
    wout_wait = load_weight(place, parts, masks, 1, wout, sems.at[nf + 1])
    acc[...] = jnp.zeros_like(acc)
    own = jnp.zeros((8, rows), F32)
    for d in range(nf):
        waits[d]()
        x = xbuf[d].astype(F32)
        inv = lax.rsqrt(jnp.mean(x * x, axis=1, keepdims=True) + EPS)
        n = (x * inv * gain[...]).astype(BF16)
        for b in range(fb):
            normed[b, d * rows : (d + 1) * rows, :] = n[:, block(b)]
            if d == 0:
                own = own + dot(three_terms(readout[:, block(b)]), xbuf[0, :, block(b)], NT)
    normed_wait = load(normed, normed_out, sems.at[nf + 2])
    win_wait()
    wout_wait()

    @loop(nj)
    def _(j):
        which = [idx[j, k] for k in range(kb)]
        picked = jnp.concatenate([normed[w] for w in which], axis=1)
        v = dot(picked, win[:, column(j)])
        v2 = v * v
        t = jnp.tanh(GELU_A * v * (1.0 + GELU_B * v2))
        half = 0.5 * (1.0 + t)
        a = (v * half).astype(BF16)
        act[j] = a
        slope = half + 0.5 * v * (1.0 - t * t) * (GELU_A * (1.0 + 3.0 * GELU_B * v2))
        dact[j] = slope.astype(BF16)
        pltpu.make_async_copy(act.at[j], act_out.at[j], sems.at[nf + 3]).start()
        pltpu.make_async_copy(dact.at[j], dact_out.at[j], sems.at[nf + 4]).start()
        terms = dot(a, wout[:, column(j)], NT)
        for k, w in enumerate(which):
            acc[w] += terms[:, block(k)]

    act_wait = pltpu.make_async_copy(act, act_out, sems.at[nf + 3]).wait
    dact_wait = pltpu.make_async_copy(dact, dact_out, sems.at[nf + 4]).wait
    spread(acc, [branch.at[d] for d in range(nf)], rows)
    waits = [load(branch.at[d], branch_out[d], sems.at[d]) for d in range(nf)]
    total = jnp.zeros((8, nf * rows), F32)
    for b in range(fb):
        total = total + dot(three_terms(readout[:, block(b)]), acc[b].astype(BF16), NT)
    own = jnp.sum(own, axis=0, keepdims=True)
    pad = jnp.zeros((1, (nf - 1) * rows), F32)
    row = jnp.sum(total, axis=0, keepdims=True) + jnp.concatenate([own, pad], axis=1)
    score[...] = jnp.concatenate([row, ids[...].astype(F32) + 1.0], axis=1)
    for wait in waits + [normed_wait, act_wait, dact_wait]:
        wait()


def store_grads(idx, place, orders, scale, pairs, keep, send):
    nj, kb = idx.shape
    count = 2 << len(orders[0])
    depth = kb * BLK // count
    per = BLK // depth
    core = place[0] & 1

    def slot(owner, order):
        m = place[0] ^ owner
        pos = 0
        for bit in order:
            pos = 2 * pos + jnp.where((m & bit) != 0, 1, 0)
        return pos * len(pairs) * depth

    def slots(own):
        return [
            jnp.where(own == 0, slot(2 * q, orders[0]), slot(2 * q, orders[1]))
            for q in range(count // 2)
        ]

    keep_at, send_at = slots(core), slots(1 - core)

    @loop(nj)
    def _(j):
        for which, (left, right) in enumerate(pairs):
            for k in range(kb):
                g = (dot(left[idx[j, k]], right[j], TN) * scale).astype(BF16)
                for half in range(per // 2):
                    q = k * (per // 2) + half
                    even = g[2 * half * depth : (2 * half + 1) * depth]
                    odd = g[(2 * half + 1) * depth : (2 * half + 2) * depth]
                    kept = pl.multiple_of(keep_at[q] + which * depth, depth)
                    sent = pl.multiple_of(send_at[q] + which * depth, depth)
                    keep[pl.ds(kept, depth), column(j)] = jnp.where(core == 0, even, odd)
                    send[pl.ds(sent, depth), column(j)] = jnp.where(core == 0, odd, even)


def upper_kernel(masks, nf, *refs):
    idx, place = refs[:2]
    ups, refs = refs[2 : 2 + nf], refs[2 + nf:]
    readout, refs = refs[0], refs[1:]
    parts, refs = refs[: len(masks)], refs[len(masks):]
    upper_out, turn, ubuf, up, wout, upper, sems = refs
    nj, kb = idx.shape
    fb = up.shape[0]
    rows = ubuf.shape[1]
    waits = [load(ups[d], ubuf.at[d], sems.at[d]) for d in range(nf)]
    wout_wait = load_weight(place, parts, masks, 1, wout, sems.at[nf])
    for d in range(nf):
        waits[d]()
        for b in range(fb):
            up[b, d * rows : (d + 1) * rows, :] = ubuf[d, :, block(b)]
    wout_wait()

    @loop(nj)
    def _(j):
        which = [idx[j, k] for k in range(kb)]
        picked = jnp.concatenate([up[w] for w in which], axis=1)
        turned = jnp.concatenate([three_terms(readout[:, column(w)]) for w in which], axis=1)
        rows_of = jnp.concatenate([picked, turned, jnp.zeros_like(turned)], axis=0)
        both = dot(rows_of, wout[:, column(j)])
        upper[j] = both[: nf * rows].astype(BF16)
        pltpu.make_async_copy(upper.at[j], upper_out.at[j], sems.at[nf + 1]).start()
        turn[:, column(j)] = jnp.sum(both[nf * rows : nf * rows + 8], axis=0, keepdims=True)

    pltpu.make_async_copy(upper, upper_out, sems.at[nf + 1]).wait()


def grads_kernel(masks, orders, scale, nf, *refs):
    idx, place, here, left, right, teacher, turn, readout, upper_in, dact_in, normed_in, act_in = refs[:12]
    ups, refs = refs[12 : 12 + nf], refs[12 + nf:]
    parts, refs = refs[: len(masks)], refs[len(masks):]
    own_coeff, pre_grad, keep, send, win, upper, dact, normed, act, cot, ubuf, sems = refs
    nj, kb = idx.shape
    rows = ubuf.shape[1]
    tokens = nf * rows
    nseg = teacher.shape[0]
    up_waits = [load(ups[d], ubuf.at[d], sems.at[4 + d]) for d in range(nf)]
    upper_wait = load(upper_in, upper, sems.at[0])
    dact_wait = load(dact_in, dact, sems.at[1])
    normed_wait = load(normed_in, normed, sems.at[2])
    act_wait = load(act_in, act, sems.at[3])
    win_wait = load_weight(place, parts, masks, 0, win, sems.at[4 + nf])
    seg = (lax.broadcasted_iota(jnp.int32, (nseg, tokens), 0) + 1).astype(F32)
    sums = jnp.zeros((nseg, 1), F32)
    counts = jnp.zeros((nseg, 1), F32)
    for group in (here, left, right):
        member = group[:, tokens:] == seg
        sums = sums + jnp.sum(jnp.where(member, group[:, :tokens], 0.0), axis=1, keepdims=True)
        counts = counts + jnp.sum(jnp.where(member, 1.0, 0.0), axis=1, keepdims=True)
    misfit = sums / jnp.maximum(counts, 1.0) - teacher[...]
    coeff = 2.0 * LOSS_WEIGHT * jnp.sum(
        jnp.where(here[:, tokens:] == seg, misfit, 0.0), axis=0, keepdims=True
    )
    across = jnp.transpose(jnp.broadcast_to(coeff, (BLK, tokens)))
    own_coeff[...] = across[:rows]
    for d in range(nf):
        up_waits[d]()
        part = across[d * rows : (d + 1) * rows]
        for b in range(cot.shape[0]):
            c = ubuf[d, :, block(b)].astype(F32) + part * readout[:, block(b)]
            cot[b, d * rows : (d + 1) * rows, :] = c.astype(BF16)
    upper_wait()
    dact_wait()

    @loop(nj)
    def _(j):
        whole = upper[j].astype(F32) + across * turn[:, column(j)]
        pre_grad[j] = (whole * dact[j].astype(F32)).astype(BF16)

    normed_wait()
    act_wait()
    store_grads(idx, place, orders, scale, ((cot, act), (normed, pre_grad)), keep, send)
    win_wait()


def back_kernel(nf, idx, pre_grad, win, *refs):
    outs, acc = refs[:nf], refs[nf]
    nj, kb = idx.shape
    acc[...] = jnp.zeros_like(acc)

    @loop(nj)
    def _(j):
        terms = dot(pre_grad[j], win[:, column(j)], NT)
        for k in range(kb):
            acc[idx[j, k]] += terms[:, block(k)]

    spread(acc, outs, outs[0].shape[0])


def finish_kernel(x_ref, gain, upstream, readout, own_coeff, own, other, out):
    x = x_ref[...].astype(F32)
    inv = lax.rsqrt(jnp.mean(x * x, axis=1, keepdims=True) + EPS)
    g = (own[...] + other[...].astype(F32)) * gain[...]
    inner = jnp.mean(g * x, axis=1, keepdims=True)
    back = inv * g - x * (inv * inv * inv) * inner
    for b in range(x.shape[1] // BLK):
        cot = upstream[:, block(b)].astype(F32) + own_coeff[...] * readout[:, block(b)]
        out[:, block(b)] = (cot.astype(BF16).astype(F32) + back[:, block(b)]).astype(BF16)


VM = pl.BlockSpec(memory_space=pltpu.VMEM)
SM = pl.BlockSpec(memory_space=pltpu.SMEM)
HBM = pl.BlockSpec(memory_space=pltpu.HBM)


def call(body, outs, args, scratch, flops):
    return pl.pallas_call(
        body,
        out_shape=[pltpu.HBM(o.shape, o.dtype) if m is HBM else o for m, o in outs],
        in_specs=[m for m, _ in args],
        out_specs=[m for m, _ in outs],
        scratch_shapes=scratch,
        compiler_params=pltpu.CompilerParams(vmem_limit_bytes=VMEM_BYTES),
        cost_estimate=pl.CostEstimate(
            flops=flops,
            bytes_accessed=sum(math.prod(o.shape) * o.dtype.itemsize for _, o in outs),
            transcendentals=0,
        ),
    )(*[pltpu.with_memory_space_constraint(a, pltpu.HBM) if m is HBM else a for m, a in args])


def stack_kernel(*refs):
    at = 0
    for p in refs[:-1]:
        refs[-1][at : at + p.shape[0]] = p[...]
        at += p.shape[0]


def stack(parts):
    rows = sum(p.shape[0] for p in parts)
    whole = jax.ShapeDtypeStruct((rows,) + parts[0].shape[1:], parts[0].dtype)
    return call(
        stack_kernel, [(VM, whole)], [(VM, p) for p in parts], [], 0
    )[0]


def swap(value, axis, mask):
    n = lax.axis_size(axis)
    return lax.ppermute(value, axis, [(i, i ^ mask) for i in range(n)])


def swap_tok(value, even, odd):
    n = lax.axis_size("tok")
    return lax.ppermute(value, "tok", [(i, i ^ (odd if i & 1 else even)) for i in range(n)])


def after(value, *others):
    return lax.optimization_barrier((value, *others))[0]


def gather_tok(w_in, w_out, bits, ties):
    held, masks = [w_in, w_out], [[(0, 0)]]
    for step, (even, odd) in enumerate(zip(bits, bits[::-1])):
        if step == 0 and len(bits) > 1:
            own = stack(held)
            held = [own] + [swap_tok(after(h, own), even, odd) for h in held]
            masks = [[(0, 0), (even, odd)]]
            continue
        if step == len(bits) - 1:
            held = [after(held[0], *ties[0])] + held[1:]
        whole = stack(held)
        flat = [m for ms in masks for m in ms]
        held = [whole, swap_tok(whole, even, odd)]
        masks = [flat, [(a ^ even, b ^ odd) for a, b in flat]]
    other = [swap(after(h, *tie), "tok", 1) for h, tie in zip(held, ties[1:])]
    return held + other, masks + [[(b ^ 1, a ^ 1) for a, b in ms] for ms in masks]


class Halving:
    def __init__(self, terms):
        self.terms = terms

    def total(self):
        return functools.reduce(lambda a, b: a + b, [t.astype(F32) for t in self.terms])

    def away(self):
        half = self.terms[0].shape[0] // 2
        sent = Halving([t[half:] for t in self.terms]).total().astype(BF16)
        self.terms = [t[:half] for t in self.terms]
        return sent

    def add(self, term):
        self.terms.append(term)


def gather_feat(own, bits, far=None):
    held = {0: own}
    for bit in bits[::-1]:
        if bit == bits[-1] and far is not None:
            held[bit] = far
        else:
            held.update({
                m ^ bit: swap(held[m] if far is None else after(held[m], far), "feat", bit)
                for m in sorted(held)
            })
    return [held[d] for d in range(2 * bits[-1])]


def scatter_near(parts):
    return {d: swap(parts[d + 1], "feat", 1) for d in range(len(parts) - 2, 0, -2)}


def scatter_far(parts, held, bits, tie):
    firsts = [held[d] for d in sorted(held)]
    held = {d: parts[d].astype(F32) + got.astype(F32) for d, got in held.items()}
    beside = swap(after(parts[1], *firsts), "feat", 1)
    held[0] = parts[0].astype(F32) + beside.astype(F32)
    for bit in bits[1:]:
        stay = [d for d in held if not d & bit]
        for d in sorted(stay, reverse=True):
            got = swap(after(held[d | bit].astype(BF16), tie), "feat", bit)
            if d == 0 and bit == bits[-1]:
                return held[0], got, beside
            held[d] = held[d] + got.astype(F32)
        held = {d: held[d] for d in stay}


def on_device(
    inputs, norm_gain, w_in, w_out, block_index, segment_ids, teacher_scores, upstream, readout
):
    rows, width = inputs.shape
    nt, nf = lax.axis_size("tok"), lax.axis_size("feat")
    nj, kb = block_index.shape
    hidden = w_in.shape[1]
    fb = width // BLK
    depth = w_in.shape[0]
    tokens = rows * nf
    grad_scale = 1.0 / math.sqrt(tokens * nt)
    bits = bits_of(nt)[1:]
    orders = (bits, bits[::-1])
    feat_bits = bits_of(nf)
    place = lax.axis_index("tok").astype(jnp.int32).reshape(1)
    gain_row, readout_row = norm_gain.reshape(1, width), readout.reshape(1, width)
    flops = 2 * tokens * hidden * kb * BLK
    sds = jax.ShapeDtypeStruct
    scalars = [(SM, block_index), (SM, place)]

    xs = gather_feat(inputs, feat_bits)
    near, far = xs[1], xs[feat_bits[-1]]
    upstream_far = swap(after(upstream, near, far), "feat", feat_bits[-1])
    ups = gather_feat(upstream, feat_bits, upstream_far)
    parts, masks = gather_tok(
        w_in, w_out, bits, ((near, far), [upstream_far], xs[2:])
    )
    parts = [(HBM, p) for p in parts]

    by_feature = pltpu.VMEM((fb, tokens, BLK), BF16)
    by_hidden = pltpu.VMEM((nj, tokens, BLK), BF16)
    weight = pltpu.VMEM((kb * BLK, hidden), BF16)
    summed = pltpu.VMEM((fb, tokens, BLK), F32)
    piece = sds((rows, width), BF16)

    outs = call(
        functools.partial(forward_kernel, masks, nf),
        [
            (HBM, sds((fb, tokens, BLK), BF16)),
            (HBM, sds((nj, tokens, BLK), BF16)),
            (HBM, sds((nj, tokens, BLK), BF16)),
            (VM, sds((1, tokens + rows), F32)),
        ]
        + [(HBM, piece)] * nf,
        scalars
        + [(HBM, x) for x in xs]
        + [(VM, gain_row), (VM, readout_row), (VM, segment_ids.reshape(1, rows))]
        + parts,
        [
            pltpu.VMEM((nf, rows, width), BF16),
            by_feature,
            by_hidden,
            by_hidden,
            weight,
            weight,
            summed,
            pltpu.VMEM((nf, rows, width), BF16),
            pltpu.SemaphoreType.DMA((nf + 5,)),
        ],
        2 * flops,
    )
    normed, act, dact, here = outs[:4]
    branch = outs[4:]

    upper, turn = call(
        functools.partial(upper_kernel, masks, nf),
        [
            (HBM, sds((nj, tokens, BLK), BF16)),
            (VM, sds((1, hidden), F32)),
        ],
        scalars + [(HBM, u) for u in ups] + [(VM, readout_row)] + parts,
        [
            pltpu.VMEM((nf, rows, width), BF16),
            by_feature,
            weight,
            by_hidden,
            pltpu.SemaphoreType.DMA((nf + 2,)),
        ],
        flops,
    )
    for step, bit in enumerate(feat_bits):
        there = swap(after(here, *ups[1:]) if step == 0 else here, "feat", bit)
        if step == 0:
            branch_near = scatter_near([after(b, there) for b in branch])
        if bit == feat_bits[-1]:
            there = after(there, turn)
        turned = jnp.flip(there[:, :tokens].reshape(nf // (2 * bit), 2, bit * rows), axis=1)
        here = jnp.concatenate(
            [here[:, :tokens] + turned.reshape(1, tokens), here[:, tokens:], there[:, tokens:]],
            axis=1,
        )
    left = swap(here, "tok", 1)
    odd = range(1, nt - 1, 2)
    right = lax.ppermute(here, "tok", [(i, i + 1) for i in odd] + [(i + 1, i) for i in odd])

    branch_near = {d: after(got, turn) for d, got in branch_near.items()}
    half_grads = sds((kb * BLK, hidden), BF16)
    own_coeff, pre_grad, keep, send, win = call(
        functools.partial(grads_kernel, masks, orders, grad_scale, nf),
        [
            (VM, sds((rows, BLK), F32)),
            (VM, sds((nj, tokens, BLK), BF16)),
            (VM, half_grads),
            (VM, half_grads),
            (VM, sds((kb * BLK, hidden), BF16)),
        ],
        scalars
        + [(VM, here), (VM, left), (VM, right), (VM, teacher_scores.reshape(-1, 1)), (VM, turn)]
        + [(VM, readout_row)]
        + [(HBM, a) for a in (upper, dact, normed, act)]
        + [(HBM, u) for u in ups]
        + parts,
        [
            by_hidden,
            by_hidden,
            by_feature,
            by_hidden,
            by_feature,
            pltpu.VMEM((nf, rows, width), BF16),
            pltpu.SemaphoreType.DMA((nf + 5,)),
        ],
        2 * flops,
    )
    back = call(
        functools.partial(back_kernel, nf),
        [(VM, piece)] * nf,
        [(SM, block_index), (VM, pre_grad), (VM, win)],
        [summed],
        flops,
    )
    branch_own, branch_got, beside = scatter_far(branch, branch_near, feat_bits, here)
    branch_got = after(branch_got, own_coeff)
    layer_out = (inputs.astype(F32) + (branch_own + branch_got.astype(F32))).astype(BF16)
    send = after(send, branch_got, beside)
    own, got, _ = scatter_far(back, scatter_near(back), feat_bits, branch_got)
    sums = Halving([keep, after(swap(send, "tok", 1), back[1])])
    for pair in zip(bits, bits[::-1]):
        sums.add(swap_tok(sums.away(), *pair))
    grads = sums.total()
    grad_out, grad_in = grads[:depth], grads[depth:]
    got = after(got, grad_out, grad_in)
    (input_grad,) = call(
        finish_kernel,
        [(VM, piece)],
        [
            (VM, a)
            for a in (inputs, gain_row, upstream, readout_row, own_coeff, own, got)
        ],
        [],
        rows * width,
    )
    return (layer_out, input_grad, grad_in, grad_out)


def solution(mesh):
    return jax.shard_map(
        on_device,
        mesh=mesh,
        in_specs=(
            P(("tok", "feat"), None),
            P(),
            P("tok", "feat"),
            P("tok", "feat"),
            P("feat", None),
            P(("tok", "feat")),
            P(),
            P(("tok", "feat"), None),
            P(),
        ),
        out_specs=(
            P(("tok", "feat"), None),
            P(("tok", "feat"), None),
            P("tok", "feat"),
            P("tok", "feat"),
        ),
        check_vma=False,
    )
```
